256 devices in a mesh: dp: 8 (over z), expert: 32 (over y, x, core).
Axes of the slice: x: 4, y: 4, z: 8, core: 2. Of those that a mesh axis runs over, the one named last changes fastest.
Arguments:
- activations: bfloat16 [32768, 2048], P(('dp', 'expert')), may hold values from -6 to 6
- expert_ids: int32 [32768, 8], P(('dp', 'expert')), may hold values from 0 to 127, all different within a row; in each aligned block of 128 rows (0 to 127, 128 to 255, ...) at most 12 rows name the same one
- route_gates: float32 [32768, 8], P(('dp', 'expert')), may hold values from 0.2 to 1
- gate_proj: bfloat16 [32, 2048, 768], P('expert'), may hold values from -0.125 to 0.125
- up_proj: bfloat16 [32, 2048, 768], P('expert'), may hold values from -0.125 to 0.125
- down_proj: bfloat16 [32, 2048, 768], P('expert'), may hold values from -0.21875 to 0.21875
- cotangent: bfloat16 [32768, 2048], P(('dp', 'expert')), may hold values from -3 to 3
Outputs:
- layer_out: bfloat16 [32768, 2048], P(('dp', 'expert'))
- grad_input: bfloat16 [32768, 2048], P(('dp', 'expert'))
- grad_gate: bfloat16 [32, 2048, 768], P('expert', 'dp')
- grad_up: bfloat16 [32, 2048, 768], P('expert', 'dp')
- grad_down: bfloat16 [32, 2048, 768], P('expert', 'dp')
The draws below stay inside these ranges and needn't reach their ends.
Inputs may be any that keep to these rules, and one draw needn't show every extreme that they name: `expert_ids`: each row names 8 different experts. Within the 128 rows of one device no expert is named by more than 12 rows; in some devices' rows an expert is named by exactly 12.
All inputs are finite; a program needn't handle non-finite values.
Results may differ from the reference program's by a relative error of at most 0.017.
Values may be sent and summed in bfloat16 or wider, within the bound.
A program may use at most 128 MiB of HBM per device.

```python
import math
import jax
import jax.numpy as jnp
import numpy as np
from jax import lax

D = 2048
FF = 768
EXPERTS = 128
TOP = 8
TOK_DEV = 128
CAP = 12
WINDOW = 32
TOKENS = 32768
N_DP = 8
N_EXPERT = 32


def levels(stream_key, shape, cuts, smallest, top_value):
    factor_of = 1.0
    for dim, shards_of in cuts:
        steps = jax.random.uniform(jax.random.fold_in(jax.random.fold_in(stream_key, 6), dim), (shards_of,), jnp.float32, smallest / len(cuts), top_value / len(cuts))
        factor_of = factor_of * jnp.repeat(jnp.exp(steps), shape[dim] // shards_of).reshape((-1,) + (1,) * (len(shape) - 1 - dim))
    return factor_of


def assign_block(own_key, own, number, rows, amount, top, reach, slope):
    ranking = jax.random.permutation(own_key, amount)
    heavy_load, common = portions_of(amount, rows * top, reach, slope, True), portions_of(amount, rows * top, reach, slope, False)
    places = jnp.arange(amount)

    def named(sizes, offset_by):
        used = int((sizes > 0).sum())
        fixed = max(1, used // 4)
        moved = fixed + (places - fixed + offset_by * (used - fixed)) % max(1, amount - fixed)
        return jnp.zeros((amount,), jnp.int32).at[ranking[jnp.where(places < fixed, places, moved)]].set(jnp.asarray(sizes, jnp.int32))

    sizes = jnp.where(number % 4 == 0, named(heavy_load, number // 4), named(common, number - number // 4 - 1))
    mixed = jax.random.permutation(jax.random.fold_in(own, 3), amount)
    donor, taker = mixed[0:amount // 2 * 2:2], mixed[1:amount // 2 * 2:2]
    room = jnp.minimum(sizes[donor] - 1, reach - sizes[taker]) // 2
    room = jnp.where((donor == ranking[0]) | (taker == ranking[0]) | (sizes[taker] == 0), 0, jnp.maximum(room, 0))
    moved = jax.random.randint(jax.random.fold_in(own, 4), (amount // 2,), 0, 1 << 20) % (room + 1)
    sizes = sizes.at[donor].add(-moved).at[taker].add(moved)
    labels = jnp.searchsorted(jnp.cumsum(sizes), jnp.arange(rows * top), side="right").astype(jnp.int32)
    listing = labels.reshape(top, rows).T
    listing = listing[jax.random.permutation(jax.random.fold_in(own, 1), rows)]
    offset_by = jax.random.randint(jax.random.fold_in(own, 2), (rows, 1), 0, top)
    return jnp.take_along_axis(listing, (jnp.arange(top)[None, :] + offset_by) % top, axis=1)


def portions_of(count, total, bound, lean, full):
    portions = [(1 << 20) // math.isqrt(grade ** lean) + 1 for grade in range(1, count + 1)]
    largest = bound if full else min(bound, max(-(-total // count), total * portions[0] // sum(portions)))
    least = 1 if total - largest >= count - 1 else 0
    counts, spare = [largest] + [least] * (count - 1), total - largest - least * (count - 1)
    while spare > 0:
        candidates = [i for i in range(1, count) if counts[i] < largest] or [i for i in range(1, count) if counts[i] < bound]
        whole, remaining = sum([portions[i] for i in candidates]), spare
        for i in candidates:
            extra = min(bound - counts[i], max(1, remaining * portions[i] // whole), spare)
            counts[i] = counts[i] + extra
            spare = spare - extra
    return np.array(counts)


def normal_values(rng, dims, spread, reach, split=(), held_as=jnp.bfloat16):
    array = spread * jax.random.normal(rng, dims, jnp.float32)
    if split:
        array = array * levels(rng, dims, split, -0.22, 0.18)
    return jnp.clip(array, -reach, reach).astype(held_as)


def setup_inputs(seed: int = 0) -> dict:
    keys = jax.random.split(jax.random.key(seed), 8)
    activations = normal_values(keys[0], (TOKENS, D), 1.0, 6.0, ((0, 256),))
    expert_ids_keys = jax.random.split(jax.random.fold_in(keys[1], 1), TOKENS // TOK_DEV)
    expert_ids_turns = jax.random.permutation(jax.random.fold_in(keys[1], 3), TOKENS // TOK_DEV)
    expert_ids = jax.vmap(lambda own, number: assign_block(jax.random.fold_in(keys[1], 2), own, number, TOK_DEV, EXPERTS, TOP, CAP, 2))(expert_ids_keys, expert_ids_turns).reshape((TOKENS, TOP))
    route_gates = jnp.clip(0.2 + 0.8 * jax.random.uniform(keys[2], (TOKENS, TOP), jnp.float32) ** levels(keys[2], (TOKENS, TOP), ((0, 256),), -0.2, 0.2), 0.2, 1.0)
    gate_proj = normal_values(keys[3], (WINDOW, D, FF), D ** -0.5, 0.125, ((0, 32),))
    up_proj = normal_values(keys[4], (WINDOW, D, FF), D ** -0.5, 0.125, ((0, 32),))
    down_proj = normal_values(keys[5], (WINDOW, D, FF), FF ** -0.5, 0.21875, ((0, 32),))
    cotangent = normal_values(keys[6], (TOKENS, D), 0.5, 3.0, ((0, 256),))
    return dict(activations=activations, expert_ids=expert_ids, route_gates=route_gates, gate_proj=gate_proj, up_proj=up_proj, down_proj=down_proj, cotangent=cotangent)


def group_sum(left_side, right_side):
    left_wide = left_side.astype(jnp.float32).reshape(N_DP, N_EXPERT * CAP, left_side.shape[1])
    right_wide = right_side.astype(jnp.float32).reshape(N_DP, N_EXPERT * CAP, right_side.shape[1])
    partial_value = jnp.einsum("grd,grf->gdf", left_wide, right_wide)
    rounded = lax.optimization_barrier(partial_value.astype(jnp.bfloat16))
    return jnp.sum(rounded.astype(jnp.float32), axis=0).astype(jnp.bfloat16)


def reference(activations, expert_ids, route_gates, gate_proj, up_proj, down_proj, cotangent):
    sources = N_DP * N_EXPERT
    buffer_rows = sources * CAP
    grouped = expert_ids.reshape(sources, TOK_DEV, TOP)
    window_range = jnp.arange(WINDOW, dtype=jnp.int32)
    onehot = (grouped[:, :, :, None] == window_range[None, None, None, :]).astype(jnp.int32)
    per_token = jnp.sum(onehot, axis=2)
    earlier = jnp.cumsum(per_token, axis=1) - per_token
    slot_pick = jnp.sum(onehot * earlier[:, :, None, :], axis=3)
    source_base = (jnp.arange(sources, dtype=jnp.int32) * CAP)[:, None, None]
    row_pick = (source_base + slot_pick).astype(jnp.int32).reshape(TOKENS, TOP)
    active = expert_ids < WINDOW

    def one_expert(expert):
        inputs = jnp.zeros((buffer_rows, D), jnp.bfloat16)
        cot_rows = jnp.zeros((buffer_rows, D), jnp.bfloat16)
        gate_rows = jnp.zeros((buffer_rows,), jnp.float32)
        for position in range(TOP):
            where_to = jnp.where(expert_ids[:, position] == expert, row_pick[:, position], buffer_rows).astype(jnp.int32)
            inputs = inputs.at[where_to].set(activations, mode="drop")
            cot_rows = cot_rows.at[where_to].set(cotangent, mode="drop")
            gate_rows = gate_rows.at[where_to].set(route_gates[:, position], mode="drop")
        gate_matrix = gate_proj[expert]
        up_matrix = up_proj[expert]
        down_matrix = down_proj[expert]
        gate_pre = jnp.dot(inputs, gate_matrix, preferred_element_type=jnp.float32)
        up_pre = jnp.dot(inputs, up_matrix, preferred_element_type=jnp.float32)
        activated = (jax.nn.silu(gate_pre) * up_pre).astype(jnp.bfloat16)
        expert_out = jnp.dot(activated, down_matrix.T, preferred_element_type=jnp.float32).astype(jnp.bfloat16)
        scaled_cot = (gate_rows[:, None] * cot_rows.astype(jnp.float32)).astype(jnp.bfloat16)
        back_act = jnp.dot(scaled_cot, down_matrix, preferred_element_type=jnp.float32)
        sigmoid_gate = jax.nn.sigmoid(gate_pre)
        grad_up_pre = (back_act * jax.nn.silu(gate_pre)).astype(jnp.bfloat16)
        grad_gate_pre = (back_act * up_pre * sigmoid_gate * (1.0 + gate_pre * (1.0 - sigmoid_gate))).astype(jnp.bfloat16)
        choice_grad = (jnp.dot(grad_gate_pre, gate_matrix.T, preferred_element_type=jnp.float32)
                       + jnp.dot(grad_up_pre, up_matrix.T, preferred_element_type=jnp.float32)).astype(jnp.bfloat16)
        return (expert_out, choice_grad, group_sum(inputs, grad_gate_pre),
                group_sum(inputs, grad_up_pre), group_sum(scaled_cot, activated))

    out_all, grad_all, grad_gate, grad_up, grad_down = lax.map(one_expert, window_range)
    out_flat = out_all.reshape(WINDOW * buffer_rows, D)
    grad_flat = grad_all.reshape(WINDOW * buffer_rows, D)
    layer_sum = jnp.zeros((TOKENS, D), jnp.float32)
    input_sum = jnp.zeros((TOKENS, D), jnp.float32)
    for position in range(TOP):
        flat_index = jnp.where(active[:, position], expert_ids[:, position] * buffer_rows + row_pick[:, position], 0).astype(jnp.int32)
        keep_mask = active[:, position][:, None]
        layer_sum = layer_sum + jnp.where(keep_mask, route_gates[:, position][:, None] * out_flat[flat_index].astype(jnp.float32), 0.0)
        input_sum = input_sum + jnp.where(keep_mask, grad_flat[flat_index].astype(jnp.float32), 0.0)
    return (layer_sum.astype(jnp.bfloat16), input_sum.astype(jnp.bfloat16), grad_gate, grad_up, grad_down)
```

```python
import functools

import jax
import jax.numpy as jnp
import numpy as np
from jax import lax
from jax.experimental import pallas as pl
from jax.experimental.pallas import tpu as pltpu
from jax.sharding import PartitionSpec as P

MESH = pl.DeviceIdType.MESH
BF16 = jnp.bfloat16
F32 = jnp.float32

CAP = 12
NE = 32
ND = 8
TOK = 128
TOP = 8
D = 2048
FF = 768
SLOTS = NE * CAP
GROUP = 8
NG = NE // GROUP
NQ = 4
QW = D // NQ
GR = GROUP * CAP
PR = CAP * NQ
DC = D // ND
HALF = FF // 2
TILE = 256


def dot(a, b):
    return jnp.dot(a, b, preferred_element_type=F32)


def dot_t(a, b):
    return lax.dot_general(a, b, (((1,), (1,)), ((), ())), preferred_element_type=F32)


def constants():
    j = np.arange(SLOTS)
    expand = (j[:, None] // CAP == np.arange(NE)[None, :]).astype(np.float32)
    slot_row = np.broadcast_to((j % CAP)[:, None], (SLOTS, TOK)).astype(np.float32)
    rows = np.arange(GROUP * PR)
    q, rest = rows // GR, rows % GR
    source = (rest // CAP) * PR + q * CAP + rest % CAP
    unshuffle = (source[:, None] == rows[None, :]).astype(np.float32)
    return (
        jnp.asarray(expand, BF16),
        jnp.asarray(slot_row, F32),
        jnp.asarray(unshuffle, BF16),
        jnp.asarray(unshuffle.T, BF16),
    )


def kernel(
    ids_ref, gates_ref, act_ref, cot_ref, wg_hbm, wu_hbm, wd_hbm, expand_ref, row_ref, un_ref, sh_ref,
    lo_ref, gi_ref, gg_ref, gu_ref, gd_ref,
    wg, wu, wd, pick, sgate, comb, send, recv, stack, x_rows, c_rows, lt, fac, hid, rs_send, rs_recv,
    wsem, lsem, ssem, rsem, zs, zr,
):
    me = lax.axis_index("expert")
    z = lax.axis_index("dp")
    my_y, my_x, my_c = me // 8, (me // 2) % 4, me % 2

    def peer(o):
        return (((my_y + o // 8) % 4) * 4 + (my_x + (o // 2) % 4) % 4) * 2 + (my_c + o % 2) % 2

    loads = [
        pltpu.make_async_copy(src.at[0], dst, wsem.at[i])
        for i, (src, dst) in enumerate(((wg_hbm, wg), (wu_hbm, wu), (wd_hbm, wd)))
    ]
    for load in loads:
        load.start()

    barrier = pltpu.get_barrier_semaphore()

    def greet(o, _):
        pl.semaphore_signal(barrier, inc=1, device_id={"expert": peer(o)}, device_id_type=MESH)
        return 0

    lax.fori_loop(1, NE, greet, 0)
    for step in (1, ND - 1):
        pl.semaphore_signal(barrier, inc=1, device_id={"dp": (z + step) % ND}, device_id_type=MESH)

    def over_peers(f):
        def body(i, _):
            f((i + 20) % NE)
            return 0

        lax.fori_loop(0, 12, body, 0)
        lax.fori_loop(13, NE, body, 0)

    def a2a(p, o):
        to = peer(o)
        return pltpu.make_async_remote_copy(
            src_ref=send.at[p, to],
            dst_ref=recv.at[p, me],
            send_sem=ssem.at[p, o],
            recv_sem=rsem.at[p, o],
            device_id={"expert": to},
            device_id_type=MESH,
        )

    def own(p):
        return pltpu.make_async_copy(send.at[p, me], recv.at[p, me], lsem.at[p])

    def ring(m, d, s):
        return pltpu.make_async_remote_copy(
            src_ref=rs_send.at[m, d, s],
            dst_ref=rs_recv.at[m, d, s],
            send_sem=zs.at[m, d, s],
            recv_sem=zr.at[m, d, s],
            device_id={"dp": (z + 1 - 2 * d + ND) % ND},
            device_id_type=MESH,
        )

    ids = ids_ref[...]
    gates = gates_ref[...]
    experts = lax.broadcasted_iota(jnp.int32, (TOK, NE), 1)
    named = jnp.zeros((TOK, NE), F32)
    gate_of = jnp.zeros((TOK, NE), F32)
    for k in range(TOP):
        hit = ids[:, k : k + 1] == experts
        named = named + jnp.where(hit, 1.0, 0.0)
        gate_of = gate_of + jnp.where(hit, gates[:, k : k + 1], 0.0)
    earlier_than = lax.broadcasted_iota(jnp.int32, (TOK, TOK), 0) > lax.broadcasted_iota(jnp.int32, (TOK, TOK), 1)
    earlier = dot(jnp.where(earlier_than, 1.0, 0.0).astype(BF16), named.astype(BF16))
    slot_of = jnp.where(named > 0.0, earlier, -1.0).astype(BF16)
    expand = expand_ref[...]
    match = dot_t(expand, slot_of) == row_ref[...]
    high = gate_of.astype(BF16)
    rest = gate_of - high.astype(F32)
    mid = rest.astype(BF16)
    low = (rest - mid.astype(F32)).astype(BF16)
    spread = dot_t(expand, high) + dot_t(expand, mid) + dot_t(expand, low)
    weight = jnp.where(match, spread, 0.0)
    ones = jnp.where(match, 1.0, 0.0)
    pick[...] = ones.astype(BF16)
    sgate[...] = jnp.sum(weight, axis=1, keepdims=True)
    weight_t = weight.T
    weight_high = weight_t.astype(BF16)
    comb[0] = weight_high
    comb[1] = (weight_t - weight_high.astype(F32)).astype(BF16)
    comb[2] = ones.T.astype(BF16)

    def shuffle_out(p, g, stacked):
        packed = dot(sh_ref[...], stacked).astype(BF16)
        send[p, g * GROUP : (g + 1) * GROUP] = packed.reshape(GROUP, PR, QW)

    def pack(p, g, source, scaled):
        rows = dot(pick[g * GR : (g + 1) * GR, :], source[...])
        if scaled:
            rows = rows * sgate[g * GR : (g + 1) * GR, :]
        rows = rows.astype(BF16)
        shuffle_out(p, g, jnp.concatenate([rows[:, q * QW : (q + 1) * QW] for q in range(NQ)], axis=0))

    def unshuffle(p, out):
        for g in range(NG):
            block = recv[p, g * GROUP : (g + 1) * GROUP].reshape(GROUP * PR, QW)
            block = dot(un_ref[...], block).astype(BF16)
            for q in range(NQ):
                out[g * GR : (g + 1) * GR, q * QW : (q + 1) * QW] = block[q * GR : (q + 1) * GR]

    for g in range(NG):
        pack(0, g, act_ref, False)
    pl.semaphore_wait(barrier, NE - 1 + 2)
    over_peers(lambda o: a2a(0, o).start())
    own(0).start()
    for g in range(NG):
        pack(1, g, cot_ref, True)

    def next_cot(o):
        a2a(0, o).wait_send()
        a2a(1, o).start()

    over_peers(next_cot)
    own(1).start()

    over_peers(lambda o: a2a(0, o).wait_recv())
    own(0).wait()
    unshuffle(0, x_rows)
    for load in loads:
        load.wait()

    def put_hidden(m, n, value):
        for at in range(n * TILE, (n + 1) * TILE, 128):
            d, col = at // HALF, at % HALF
            hid[m, d, :, col : col + 128] = value[:, at - n * TILE : at - n * TILE + 128]

    for n in range(FF // TILE):
        cols = slice(n * TILE, (n + 1) * TILE)
        gate_pre = dot(x_rows[...], wg[:, cols])
        up_pre = dot(x_rows[...], wu[:, cols])
        sig = 1.0 / (1.0 + jnp.exp(-gate_pre))
        silu = gate_pre * sig
        fac[0, :, cols] = silu
        fac[1, :, cols] = up_pre * sig * (1.0 + gate_pre * (1.0 - sig))
        put_hidden(0, n, (silu * up_pre).astype(BF16))

    for j in range(ND):
        lt[1, j] = x_rows[:, j * DC : (j + 1) * DC].T

    def whole(m):
        return jnp.concatenate([hid[m, 0], hid[m, 1]], axis=1)

    def send_back(p, q, rows):
        for g in range(NG):
            stack[g, q * GR : (q + 1) * GR] = rows[g * GR : (g + 1) * GR].astype(BF16)

    for q in range(NQ):
        send_back(2, q, dot_t(whole(0), wd[q * QW : (q + 1) * QW, :]))
    for g in range(NG):
        shuffle_out(2, g, stack[g])

    over_peers(lambda o: a2a(1, o).wait_recv())
    own(1).wait()
    unshuffle(1, c_rows)
    for j in range(ND):
        lt[0, j] = c_rows[:, j * DC : (j + 1) * DC].T

    def chunk(d, s):
        return (z - (1 - 2 * d) * (1 + s) + 2 * ND) % ND

    def part(m, d, c):
        return dot(lt[(m + 1) // 2, c], hid[m, d])

    def first(m):
        for d in range(2):
            rs_send[m, d, 0] = part(m, d, chunk(d, 0)).astype(BF16)
            ring(m, d, 0).start()

    def steps(lowest, end):
        def body(i, _):
            s, m, d = i // 6, (i // 2) % 3, i % 2
            mine = part(m, d, chunk(d, s))
            ring(m, d, s - 1).wait_recv()
            rs_send[m, d, s] = (mine + rs_recv[m, d, s - 1].astype(F32)).astype(BF16)
            ring(m, d, s).start()
            return 0

        lax.fori_loop(6 * lowest, 6 * end, body, 0)

    first(0)
    over_peers(lambda o: a2a(2, o).start())
    own(2).start()

    for n in range(FF // TILE):
        cols = slice(n * TILE, (n + 1) * TILE)
        back = dot(c_rows[...], wd[:, cols])
        put_hidden(2, n, (back * fac[0, :, cols]).astype(BF16))
        put_hidden(1, n, (back * fac[1, :, cols]).astype(BF16))
    first(1)
    first(2)
    steps(1, 2)

    for q in range(NQ):
        rows = slice(q * QW, (q + 1) * QW)
        send_back(3, q, dot_t(whole(1), wg[rows, :]) + dot_t(whole(2), wu[rows, :]))
    for g in range(NG):
        shuffle_out(3, g, stack[g])
    over_peers(lambda o: a2a(3, o).start())
    own(3).start()

    steps(2, 4)
    over_peers(lambda o: a2a(2, o).wait_recv())
    own(2).wait()
    unshuffle(2, x_rows)
    for q in range(NQ):
        cols = slice(q * QW, (q + 1) * QW)
        lo_ref[:, cols] = (dot(comb[0], x_rows[:, cols]) + dot(comb[1], x_rows[:, cols])).astype(BF16)

    steps(4, 6)
    over_peers(lambda o: a2a(3, o).wait_recv())
    own(3).wait()
    unshuffle(3, x_rows)
    for q in range(NQ):
        cols = slice(q * QW, (q + 1) * QW)
        gi_ref[:, cols] = dot(comb[2], x_rows[:, cols]).astype(BF16)

    steps(6, 7)
    for m, out in ((0, gd_ref), (1, gg_ref), (2, gu_ref)):
        for d in range(2):
            mine = part(m, d, z)
            ring(m, d, ND - 2).wait_recv()
            out[:, d * HALF : (d + 1) * HALF] = (mine + rs_recv[m, d, ND - 2].astype(F32)).astype(BF16)

    for p in (1, 2, 3):
        over_peers(lambda o: a2a(p, o).wait_send())

    def drain(i, _):
        ring((i // 2) % 3, i % 2, i // 6).wait_send()
        return 0

    lax.fori_loop(0, 6 * (ND - 1), drain, 0)


def shards(activations, expert_ids, route_gates, gate_proj, up_proj, down_proj, cotangent):
    vmem = pl.BlockSpec(memory_space=pltpu.VMEM)
    anywhere = pl.BlockSpec(memory_space=pl.ANY)
    dma = pltpu.SemaphoreType.DMA
    out = pl.pallas_call(
        kernel,
        out_shape=(
            jax.ShapeDtypeStruct((TOK, D), BF16),
            jax.ShapeDtypeStruct((TOK, D), BF16),
            jax.ShapeDtypeStruct((DC, FF), BF16),
            jax.ShapeDtypeStruct((DC, FF), BF16),
            jax.ShapeDtypeStruct((DC, FF), BF16),
        ),
        in_specs=[vmem] * 4 + [anywhere] * 3 + [vmem] * 4,
        out_specs=(vmem,) * 5,
        scratch_shapes=[
            pltpu.VMEM((D, FF), BF16),
            pltpu.VMEM((D, FF), BF16),
            pltpu.VMEM((D, FF), BF16),
            pltpu.VMEM((SLOTS, TOK), BF16),
            pltpu.VMEM((SLOTS, 1), F32),
            pltpu.VMEM((3, TOK, SLOTS), BF16),
            pltpu.VMEM((4, NE, PR, QW), BF16),
            pltpu.VMEM((4, NE, PR, QW), BF16),
            pltpu.VMEM((NG, GROUP * PR, QW), BF16),
            pltpu.VMEM((SLOTS, D), BF16),
            pltpu.VMEM((SLOTS, D), BF16),
            pltpu.VMEM((2, ND, DC, SLOTS), BF16),
            pltpu.VMEM((2, SLOTS, FF), F32),
            pltpu.VMEM((3, 2, SLOTS, HALF), BF16),
            pltpu.VMEM((3, 2, ND - 1, DC, HALF), BF16),
            pltpu.VMEM((3, 2, ND - 1, DC, HALF), BF16),
            dma((3,)),
            dma((4,)),
            dma((4, NE)),
            dma((4, NE)),
            dma((3, 2, ND - 1)),
            dma((3, 2, ND - 1)),
        ],
        compiler_params=pltpu.CompilerParams(
            collective_id=0, has_side_effects=True, vmem_limit_bytes=60 * 2**20
        ),
        cost_estimate=pl.CostEstimate(flops=12 * 10**9, bytes_accessed=15 * 10**6, transcendentals=300000),
        name="expert_layer",
    )(expert_ids, route_gates, activations, cotangent, gate_proj, up_proj, down_proj, *constants())
    layer_out, grad_input, grad_gate, grad_up, grad_down = out
    return (layer_out, grad_input, grad_gate[None], grad_up[None], grad_down[None])


def solution(mesh):
    in_specs = (
        P(("dp", "expert"), None),
        P(("dp", "expert"), None),
        P(("dp", "expert"), None),
        P("expert", None, None),
        P("expert", None, None),
        P("expert", None, None),
        P(("dp", "expert"), None),
    )
    out_specs = (
        P(("dp", "expert"), None),
        P(("dp", "expert"), None),
        P("expert", "dp", None),
        P("expert", "dp", None),
        P("expert", "dp", None),
    )
    return jax.shard_map(shards, mesh=mesh, in_specs=in_specs, out_specs=out_specs, check_vma=False)
```

```python
import functools

import jax
import jax.numpy as jnp
import numpy as np
from jax import lax
from jax.experimental import pallas as pl
from jax.experimental.pallas import tpu as pltpu
from jax.sharding import PartitionSpec as P

MESH = pl.DeviceIdType.MESH
BF16 = jnp.bfloat16
F32 = jnp.float32

CAP = 12
NE = 32
ND = 8
TOK = 128
TOP = 8
D = 2048
FF = 768
SLOTS = NE * CAP
GROUP = 8
NG = NE // GROUP
NQ = 4
QW = D // NQ
GR = GROUP * CAP
PIECE = 16
NP = CAP * NQ // PIECE
DC = D // ND
HALF = FF // 2
TILE = 256


def dot(a, b):
    return jnp.dot(a, b, preferred_element_type=F32)


def dot_t(a, b):
    return lax.dot_general(a, b, (((1,), (1,)), ((), ())), preferred_element_type=F32)


def constants():
    table = np.zeros((NP, GROUP * PIECE, 2 * GR), np.float32)
    for p in range(NP):
        for s in range(GROUP):
            for u in range(PIECE):
                q, r = divmod(p * PIECE + u, CAP)
                table[p, s * PIECE + u, (q - p) * GR + s * CAP + r] = 1.0
    return jnp.asarray(table, BF16), jnp.asarray(table.transpose(0, 2, 1), BF16)


def kernel(
    ids_ref, gates_ref, act_hbm, cot_hbm, wg_hbm, wu_hbm, wd_hbm, to_hbm, from_hbm,
    lo_hbm, gi_hbm, gg_hbm, gu_hbm, gd_hbm,
    act, cot, wg, wu, wd, to_piece, from_piece, pick, sgate, comb, send, recv, stack, x_rows, c_rows,
    lt, fac, hid, rs_send, rs_recv, tokens_out, grads_out,
    wsem, osem, lsem, ssem, rsem, csem, crem, zs, zr,
):
    me = lax.axis_index("expert")
    z = lax.axis_index("dp")
    my_y, my_x, my_c = me // 8, (me // 2) % 4, me % 2

    def peer(o):
        return (((my_y + o // 8) % 4) * 4 + (my_x + (o // 2) % 4) % 4) * 2 + (my_c + o % 2) % 2

    barrier = pltpu.get_barrier_semaphore()

    def greet(o, _):
        pl.semaphore_signal(barrier, inc=1, device_id={"expert": peer(o)}, device_id_type=MESH)
        return 0

    lax.fori_loop(1, NE, greet, 0)
    for step in (1, ND - 1):
        pl.semaphore_signal(barrier, inc=1, device_id={"dp": (z + step) % ND}, device_id_type=MESH)

    sources = (
        (act_hbm, act), (to_hbm, to_piece), (cot_hbm, cot), (from_hbm, from_piece),
        (wg_hbm.at[0], wg), (wu_hbm.at[0], wu), (wd_hbm.at[0], wd),
    )
    loads = [pltpu.make_async_copy(a, b, wsem.at[i]) for i, (a, b) in enumerate(sources)]
    for load in loads:
        load.start()

    def over_peers(f):
        def body(i, _):
            f((i + 20) % NE)
            return 0

        lax.fori_loop(0, 12, body, 0)
        lax.fori_loop(13, NE, body, 0)

    def a2a(p, o):
        to = peer(o)
        return pltpu.make_async_remote_copy(
            src_ref=send.at[p, to],
            dst_ref=recv.at[p, me],
            send_sem=ssem.at[p, o],
            recv_sem=rsem.at[p, o],
            device_id={"expert": to},
            device_id_type=MESH,
        )

    def a2a_piece(t, o):
        to = peer(o)
        return pltpu.make_async_remote_copy(
            src_ref=send.at[1, to, t],
            dst_ref=recv.at[1, me, t],
            send_sem=csem.at[t, o],
            recv_sem=crem.at[t, o],
            device_id={"expert": to},
            device_id_type=MESH,
        )

    def own(p):
        return pltpu.make_async_copy(send.at[p, me], recv.at[p, me], lsem.at[p])

    def ring(m, d, s):
        return pltpu.make_async_remote_copy(
            src_ref=rs_send.at[m, d, s],
            dst_ref=rs_recv.at[m, d, s],
            send_sem=zs.at[m, d, s],
            recv_sem=zr.at[m, d, s],
            device_id={"dp": (z + 1 - 2 * d + ND) % ND},
            device_id_type=MESH,
        )

    def chunk(d, s):
        return (z - (1 - 2 * d) * (1 + s) + 2 * ND) % ND

    chunks = [(chunk(0, i), chunk(1, i) if i < NQ - 1 else z) for i in range(NQ)]

    ids = ids_ref[...]
    gates = gates_ref[...]
    experts = lax.broadcasted_iota(jnp.int32, (NE, TOK), 0)
    named = jnp.zeros((NE, TOK), F32)
    gate_of = jnp.zeros((NE, TOK), F32)
    for k in range(TOP):
        hit = ids[k : k + 1, :] == experts
        named = named + jnp.where(hit, 1.0, 0.0)
        gate_of = gate_of + jnp.where(hit, gates[k : k + 1, :], 0.0)
    before = lax.broadcasted_iota(jnp.int32, (TOK, TOK), 0) < lax.broadcasted_iota(jnp.int32, (TOK, TOK), 1)
    earlier = dot(named.astype(BF16), jnp.where(before, 1.0, 0.0).astype(BF16))
    slot_of = jnp.where(named > 0.0, earlier, -1.0).astype(BF16)
    slots = lax.broadcasted_iota(jnp.int32, (SLOTS, NE), 0)
    first_slot = lax.broadcasted_iota(jnp.int32, (SLOTS, NE), 1) * CAP
    expand = jnp.where((slots >= first_slot) & (slots < first_slot + CAP), 1.0, 0.0)
    row = jnp.sum(expand * (slots - first_slot).astype(F32), axis=1, keepdims=True)
    expand = expand.astype(BF16)
    match = dot(expand, slot_of) == row
    high = gate_of.astype(BF16)
    rest = gate_of - high.astype(F32)
    mid = rest.astype(BF16)
    low = (rest - mid.astype(F32)).astype(BF16)
    ones = jnp.where(match, 1.0, 0.0)
    pick[...] = ones.astype(BF16)

    def shuffle_out(p, g, block):
        for t in range(NP):
            both = jnp.concatenate([block(t), block(t + 1)], axis=0)
            packed = dot(to_piece[t], both).astype(BF16)
            send[p, g * GROUP : (g + 1) * GROUP, t] = packed.reshape(GROUP, PIECE, QW)

    def unshuffle(p, q):
        out = []
        for g in range(NG):
            def piece(t):
                return recv[p, g * GROUP : (g + 1) * GROUP, t].reshape(GROUP * PIECE, QW)

            total = None
            if q < NP:
                total = dot(from_piece[q, :GR, :], piece(q))
            if q > 0:
                more = dot(from_piece[q - 1, GR:, :], piece(q - 1))
                total = more if total is None else total + more
            out.append(total.astype(BF16))
        return out

    def unshuffle_all(p):
        for q in range(NQ):
            for g, rows in enumerate(unshuffle(p, q)):
                x_rows[g * GR : (g + 1) * GR, q * QW : (q + 1) * QW] = rows

    loads[0].wait()
    loads[1].wait()
    for g in range(NG):
        rows = dot(pick[g * GR : (g + 1) * GR, :], act[...]).astype(BF16)
        shuffle_out(0, g, lambda q: rows[:, q * QW : (q + 1) * QW])
    pl.semaphore_wait(barrier, NE - 1 + 2)
    over_peers(lambda o: a2a(0, o).start())
    own(0).start()

    spread = dot(expand, high) + dot(expand, mid) + dot(expand, low)
    weight = jnp.where(match, spread, 0.0)
    sgate[...] = jnp.sum(weight, axis=1, keepdims=True)
    weight_t = weight.T
    weight_high = weight_t.astype(BF16)
    comb[0] = weight_high
    comb[1] = (weight_t - weight_high.astype(F32)).astype(BF16)
    comb[2] = ones.T.astype(BF16)

    loads[2].wait()
    for g in range(NG):
        def scaled(i):
            cols = [
                dot(pick[g * GR : (g + 1) * GR, :], cot[:, pl.ds(pl.multiple_of(c * DC, DC), DC)])
                for c in chunks[i]
            ]
            return (jnp.concatenate(cols, axis=1) * sgate[g * GR : (g + 1) * GR, :]).astype(BF16)

        blocks = [scaled(i) for i in range(NQ)]
        shuffle_out(1, g, lambda q: blocks[q])
    own(1).start()

    def next_cot(o):
        a2a(0, o).wait_send()
        a2a_piece(0, o).start()

    over_peers(next_cot)

    for load in loads[3:]:
        load.wait()
    over_peers(lambda o: a2a(0, o).wait_recv())
    own(0).wait()
    unshuffle_all(0)

    def put_hidden(m, n, value):
        for at in range(n * TILE, (n + 1) * TILE, 128):
            d, col = at // HALF, at % HALF
            hid[m, d, :, col : col + 128] = value[:, at - n * TILE : at - n * TILE + 128]

    for n in range(FF // TILE):
        cols = slice(n * TILE, (n + 1) * TILE)
        gate_pre = dot(x_rows[...], wg[:, cols])
        up_pre = dot(x_rows[...], wu[:, cols])
        sig = 1.0 / (1.0 + jnp.exp(-gate_pre))
        silu = gate_pre * sig
        fac[0, :, cols] = silu
        fac[1, :, cols] = up_pre * sig * (1.0 + gate_pre * (1.0 - sig))
        put_hidden(0, n, (silu * up_pre).astype(BF16))

    over_peers(lambda o: a2a_piece(1, o).start())

    def take_cot(i):
        for g, rows in enumerate(unshuffle(1, i)):
            for h, c in enumerate(chunks[i]):
                at = pl.ds(pl.multiple_of(c * DC, DC), DC)
                c_rows[g * GR : (g + 1) * GR, at] = rows[:, h * DC : (h + 1) * DC]
        for c in chunks[i]:
            lt[0, c] = c_rows[:, pl.ds(pl.multiple_of(c * DC, DC), DC)].T

    def part(m, d, c):
        return dot(lt[(m + 1) // 2, c], hid[m, d])

    def first(m):
        for d in range(2):
            rs_send[m, d, 0] = part(m, d, chunk(d, 0)).astype(BF16)
            ring(m, d, 0).start()

    def next_step(m, d, s):
        mine = part(m, d, chunk(d, s))
        ring(m, d, s - 1).wait_recv()
        rs_send[m, d, s] = (mine + rs_recv[m, d, s - 1].astype(F32)).astype(BF16)
        ring(m, d, s).start()

    def down_step(s):
        def body(d, _):
            next_step(0, d, s)
            return 0

        lax.fori_loop(0, 2, body, 0)

    def rounds(start, end):
        def body(i, _):
            m = (i // 2) % 3
            next_step(m, i % 2, 1 + i // 6 + 3 * ((2 - m) // 2))
            return 0

        lax.fori_loop(6 * start, 6 * end, body, 0)

    def late_rounds(start, end):
        def body(i, _):
            next_step(1 + (i // 2) % 2, i % 2, 1 + i // 4)
            return 0

        lax.fori_loop(4 * start, 4 * end, body, 0)

    over_peers(lambda o: a2a_piece(0, o).wait_recv())
    own(1).wait()
    take_cot(0)
    first(0)
    over_peers(lambda o: a2a_piece(2, o).start())

    def whole(m):
        return jnp.concatenate([hid[m, 0], hid[m, 1]], axis=1)

    def stack_rows(q, rows):
        for g in range(NG):
            stack[g, q] = rows[g * GR : (g + 1) * GR].astype(BF16)

    for q in range(NQ):
        stack_rows(q, dot_t(whole(0), wd[q * QW : (q + 1) * QW, :]))
    for g in range(NG):
        shuffle_out(2, g, lambda q: stack[g, q])

    over_peers(lambda o: a2a_piece(1, o).wait_recv())
    take_cot(1)
    down_step(1)
    for j in range(ND):
        lt[1, j] = x_rows[:, j * DC : (j + 1) * DC].T
    over_peers(lambda o: a2a_piece(2, o).wait_recv())
    take_cot(2)
    take_cot(3)
    over_peers(lambda o: a2a(2, o).start())
    own(2).start()
    down_step(2)

    for n in range(FF // TILE):
        cols = slice(n * TILE, (n + 1) * TILE)
        back = dot(c_rows[...], wd[:, cols])
        put_hidden(2, n, (back * fac[0, :, cols]).astype(BF16))
        put_hidden(1, n, (back * fac[1, :, cols]).astype(BF16))
    first(1)
    first(2)
    down_step(3)

    for q in range(NQ):
        rows = slice(q * QW, (q + 1) * QW)
        stack_rows(q, dot_t(whole(1), wg[rows, :]) + dot_t(whole(2), wu[rows, :]))
    for g in range(NG):
        shuffle_out(3, g, lambda q: stack[g, q])
    over_peers(lambda o: a2a(3, o).start())
    own(3).start()

    rounds(0, 2)
    over_peers(lambda o: a2a(2, o).wait_recv())
    own(2).wait()
    unshuffle_all(2)
    for q in range(NQ):
        cols = slice(q * QW, (q + 1) * QW)
        tokens_out[0, :, cols] = (dot(comb[0], x_rows[:, cols]) + dot(comb[1], x_rows[:, cols])).astype(BF16)
    stores = [pltpu.make_async_copy(tokens_out.at[0], lo_hbm, osem.at[0])]
    stores[0].start()

    rounds(2, 3)
    over_peers(lambda o: a2a(3, o).wait_recv())
    own(3).wait()
    unshuffle_all(3)
    for q in range(NQ):
        cols = slice(q * QW, (q + 1) * QW)
        tokens_out[1, :, cols] = dot(comb[2], x_rows[:, cols]).astype(BF16)
    stores.append(pltpu.make_async_copy(tokens_out.at[1], gi_hbm, osem.at[1]))
    stores[1].start()

    def finish(m, out):
        for d in range(2):
            mine = part(m, d, z)
            ring(m, d, ND - 2).wait_recv()
            total = mine + rs_recv[m, d, ND - 2].astype(F32)
            grads_out[m, :, d * HALF : (d + 1) * HALF] = total.astype(BF16)
        stores.append(pltpu.make_async_copy(grads_out.at[m], out, osem.at[2 + m]))
        stores[-1].start()

    late_rounds(3, 4)
    finish(0, gd_hbm)
    late_rounds(4, 6)
    for p in (2, 3):
        over_peers(lambda o: a2a(p, o).wait_send())
    for t in range(NP):
        over_peers(lambda o: a2a_piece(t, o).wait_send())
    finish(1, gg_hbm)
    finish(2, gu_hbm)

    def drain(i, _):
        ring((i // 2) % 3, i % 2, i // 6).wait_send()
        return 0

    lax.fori_loop(0, 6 * (ND - 1), drain, 0)
    for store in stores:
        store.wait()


def place(*refs):
    ins, outs, held, (in_sem, out_sem) = refs[:5], refs[5:10], refs[10:15], refs[15:]
    loads = [pltpu.make_async_copy(ins[i], held[i], in_sem.at[i]) for i in range(5)]
    stores = [
        pltpu.make_async_copy(held[i], outs[i] if i < 2 else outs[i].at[0], out_sem.at[i]) for i in range(5)
    ]
    for load in loads:
        load.start()
    for load, store in zip(loads, stores):
        load.wait()
        store.start()
    for store in stores:
        store.wait()


def shards(activations, expert_ids, route_gates, gate_proj, up_proj, down_proj, cotangent):
    vmem = pl.BlockSpec(memory_space=pltpu.VMEM)
    anywhere = pl.BlockSpec(memory_space=pl.ANY)
    dma = pltpu.SemaphoreType.DMA
    tokens = jax.ShapeDtypeStruct((TOK, D), BF16)
    grads = jax.ShapeDtypeStruct((DC, FF), BF16)
    out = pl.pallas_call(
        kernel,
        out_shape=(tokens,) * 2 + (grads,) * 3,
        in_specs=[vmem] * 2 + [anywhere] * 7,
        out_specs=(anywhere,) * 5,
        scratch_shapes=[
            pltpu.VMEM((TOK, D), BF16),
            pltpu.VMEM((TOK, D), BF16),
            pltpu.VMEM((D, FF), BF16),
            pltpu.VMEM((D, FF), BF16),
            pltpu.VMEM((D, FF), BF16),
            pltpu.VMEM((NP, GROUP * PIECE, 2 * GR), BF16),
            pltpu.VMEM((NP, 2 * GR, GROUP * PIECE), BF16),
            pltpu.VMEM((SLOTS, TOK), BF16),
            pltpu.VMEM((SLOTS, 1), F32),
            pltpu.VMEM((3, TOK, SLOTS), BF16),
            pltpu.VMEM((4, NE, NP, PIECE, QW), BF16),
            pltpu.VMEM((4, NE, NP, PIECE, QW), BF16),
            pltpu.VMEM((NG, NQ, GR, QW), BF16),
            pltpu.VMEM((SLOTS, D), BF16),
            pltpu.VMEM((SLOTS, D), BF16),
            pltpu.VMEM((2, ND, DC, SLOTS), BF16),
            pltpu.VMEM((2, SLOTS, FF), F32),
            pltpu.VMEM((3, 2, SLOTS, HALF), BF16),
            pltpu.VMEM((3, 2, ND - 1, DC, HALF), BF16),
            pltpu.VMEM((3, 2, ND - 1, DC, HALF), BF16),
            pltpu.VMEM((2, TOK, D), BF16),
            pltpu.VMEM((3, DC, FF), BF16),
            dma((7,)),
            dma((5,)),
            dma((4,)),
            dma((4, NE)),
            dma((4, NE)),
            dma((NP, NE)),
            dma((NP, NE)),
            dma((3, 2, ND - 1)),
            dma((3, 2, ND - 1)),
        ],
        compiler_params=pltpu.CompilerParams(
            collective_id=0, has_side_effects=True, vmem_limit_bytes=60 * 2**20
        ),
        cost_estimate=pl.CostEstimate(flops=12 * 10**9, bytes_accessed=15 * 10**6, transcendentals=300000),
        name="expert_layer",
    )(expert_ids.T, route_gates.T, activations, cotangent, gate_proj, up_proj, down_proj, *constants())
    kept = jax.ShapeDtypeStruct((1, DC, FF), BF16)
    return pl.pallas_call(
        place,
        out_shape=(tokens,) * 2 + (kept,) * 3,
        in_specs=[anywhere] * 5,
        out_specs=(anywhere,) * 5,
        scratch_shapes=[pltpu.VMEM(s.shape, BF16) for s in (tokens,) * 2 + (grads,) * 3] + [dma((5,)), dma((5,))],
        name="place",
    )(*out)


def solution(mesh):
    in_specs = (
        P(("dp", "expert"), None),
        P(("dp", "expert"), None),
        P(("dp", "expert"), None),
        P("expert", None, None),
        P("expert", None, None),
        P("expert", None, None),
        P(("dp", "expert"), None),
    )
    out_specs = (
        P(("dp", "expert"), None),
        P(("dp", "expert"), None),
        P("expert", "dp", None),
        P("expert", "dp", None),
        P("expert", "dp", None),
    )
    return jax.shard_map(shards, mesh=mesh, in_specs=in_specs, out_specs=out_specs, check_vma=False)
```

```python
import functools

import jax
import jax.numpy as jnp
import numpy as np
from jax import lax
from jax.experimental import pallas as pl
from jax.experimental.pallas import tpu as pltpu
from jax.sharding import PartitionSpec as P

MESH = pl.DeviceIdType.MESH
BF16 = jnp.bfloat16
F32 = jnp.float32

CAP = 12
NE = 32
ND = 8
TOK = 128
TOP = 8
D = 2048
FF = 768
SLOTS = NE * CAP
GROUP = 8
NG = NE // GROUP
NQ = 4
QW = D // NQ
GR = GROUP * CAP
PIECE = 16
NP = CAP * NQ // PIECE
STAGES = ((0, 1), (1, 3), (3, 6))
OFFSETS = (4, 3, -3, 2, -2, 1, -1, 0)
LINKS = ND - 1
DC = D // ND
HALF = FF // 2
TILE = 256


def dot(a, b):
    return jnp.dot(a, b, preferred_element_type=F32)


def dot_t(a, b):
    return lax.dot_general(a, b, (((1,), (1,)), ((), ())), preferred_element_type=F32)


def constants():
    table = np.zeros((NP, GROUP * PIECE, 2 * GR), np.float32)
    for p in range(NP):
        for s in range(GROUP):
            for u in range(PIECE):
                q, r = divmod(p * PIECE + u, CAP)
                table[p, s * PIECE + u, (q - p) * GR + s * CAP + r] = 1.0
    return jnp.asarray(table, BF16), jnp.asarray(table.transpose(0, 2, 1), BF16)


def kernel(
    ids_hbm, gates_hbm, act_hbm, cot_hbm, wg_hbm, wu_hbm, wd_hbm, to_hbm, from_hbm,
    lo_ref, gi_ref, gg_ref, gu_ref, gd_ref,
    ids_ref, gates_ref, act, cot, wg, wu, wd, to_piece, from_piece, pick, sgate, comb, send, recv, c_send, c_recv, stack, x_rows, c_rows,
    lt, fac, hid, rs_send, rs_recv,
    wsem, lsem, ssem, rsem, csem, crem, zs, zr,
):
    me = lax.axis_index("expert")
    z = lax.axis_index("dp")
    my_y, my_x, my_c = me // 8, (me // 2) % 4, me % 2

    def peer(o):
        return (((my_y + o // 8) % 4) * 4 + (my_x + (o // 2) % 4) % 4) * 2 + (my_c + o % 2) % 2

    sources = (
        (ids_hbm, ids_ref), (gates_hbm, gates_ref), (act_hbm, act), (to_hbm, to_piece), (cot_hbm, cot),
        (from_hbm, from_piece), (wg_hbm.at[0], wg), (wu_hbm.at[0], wu), (wd_hbm.at[0], wd),
    )
    loads = [pltpu.make_async_copy(a, b, wsem.at[i]) for i, (a, b) in enumerate(sources)]
    for load in loads[:4]:
        load.start()

    barrier = pltpu.get_barrier_semaphore()

    def greet(o, _):
        pl.semaphore_signal(barrier, inc=1, device_id={"expert": peer(o)}, device_id_type=MESH)
        return 0

    lax.fori_loop(1, NE, greet, 0)
    for step in (1, ND - 1):
        pl.semaphore_signal(barrier, inc=1, device_id={"dp": (z + step) % ND}, device_id_type=MESH)
    for load in loads[4:]:
        load.start()

    def over_peers(f):
        def body(i, _):
            f((i + 20) % NE)
            return 0

        lax.fori_loop(0, 12, body, 0)
        lax.fori_loop(13, NE, body, 0)

    def a2a(p, o):
        to = peer(o)
        return pltpu.make_async_remote_copy(
            src_ref=send.at[p, to],
            dst_ref=recv.at[p, me],
            send_sem=ssem.at[p, o],
            recv_sem=rsem.at[p, o],
            device_id={"expert": to},
            device_id_type=MESH,
        )

    def a2a_cot(t, o):
        to = peer(o)
        start, end = STAGES[t]
        pieces = pl.ds(start, end - start)
        return pltpu.make_async_remote_copy(
            src_ref=c_send.at[to, pieces],
            dst_ref=c_recv.at[me, pieces],
            send_sem=csem.at[t, o],
            recv_sem=crem.at[t, o],
            device_id={"expert": to},
            device_id_type=MESH,
        )

    def own(p):
        return pltpu.make_async_copy(send.at[p, me], recv.at[p, me], lsem.at[p])

    own_cot = pltpu.make_async_copy(c_send.at[me], c_recv.at[me], lsem.at[3])

    def link(m, d, i):
        return pltpu.make_async_remote_copy(
            src_ref=rs_send.at[m, d, i],
            dst_ref=rs_recv.at[m, d, i],
            send_sem=zs.at[m, d, i],
            recv_sem=zr.at[m, d, i],
            device_id={"dp": (z + 1 - 2 * d + ND) % ND},
            device_id_type=MESH,
        )

    chunks = [(z + off + ND) % ND for off in OFFSETS]

    loads[0].wait()
    loads[1].wait()
    ids = ids_ref[...]
    gates = gates_ref[...]
    experts = lax.broadcasted_iota(jnp.int32, (NE, TOK), 0)
    named = jnp.zeros((NE, TOK), F32)
    gate_of = jnp.zeros((NE, TOK), F32)
    for k in range(TOP):
        hit = ids[k : k + 1, :] == experts
        named = named + jnp.where(hit, 1.0, 0.0)
        gate_of = gate_of + jnp.where(hit, gates[k : k + 1, :], 0.0)
    before = lax.broadcasted_iota(jnp.int32, (TOK, TOK), 0) < lax.broadcasted_iota(jnp.int32, (TOK, TOK), 1)
    earlier = dot(named.astype(BF16), jnp.where(before, 1.0, 0.0).astype(BF16))
    slot_of = jnp.where(named > 0.0, earlier, -1.0).astype(BF16)
    slots = lax.broadcasted_iota(jnp.int32, (SLOTS, NE), 0)
    first_slot = lax.broadcasted_iota(jnp.int32, (SLOTS, NE), 1) * CAP
    expand = jnp.where((slots >= first_slot) & (slots < first_slot + CAP), 1.0, 0.0)
    row = jnp.sum(expand * (slots - first_slot).astype(F32), axis=1, keepdims=True)
    expand = expand.astype(BF16)
    match = dot(expand, slot_of) == row
    high = gate_of.astype(BF16)
    rest = gate_of - high.astype(F32)
    mid = rest.astype(BF16)
    low = (rest - mid.astype(F32)).astype(BF16)
    ones = jnp.where(match, 1.0, 0.0)
    pick[...] = ones.astype(BF16)

    def shuffle_out(p, g, block):
        for t in range(NP):
            both = jnp.concatenate([block(t), block(t + 1)], axis=0)
            packed = dot(to_piece[t], both).astype(BF16)
            send[p, g * GROUP : (g + 1) * GROUP, t] = packed.reshape(GROUP, PIECE, QW)

    def unshuffle(p, q):
        out = []
        for g in range(NG):
            def piece(t):
                return recv[p, g * GROUP : (g + 1) * GROUP, t].reshape(GROUP * PIECE, QW)

            total = None
            if q < NP:
                total = dot(from_piece[q, :GR, :], piece(q))
            if q > 0:
                more = dot(from_piece[q - 1, GR:, :], piece(q - 1))
                total = more if total is None else total + more
            out.append(total.astype(BF16))
        return out

    def unshuffle_all(p):
        for q in range(NQ):
            for g, rows in enumerate(unshuffle(p, q)):
                x_rows[g * GR : (g + 1) * GR, q * QW : (q + 1) * QW] = rows

    loads[2].wait()
    loads[3].wait()
    for g in range(NG):
        rows = dot(pick[g * GR : (g + 1) * GR, :], act[...]).astype(BF16)
        shuffle_out(0, g, lambda q: rows[:, q * QW : (q + 1) * QW])
    pl.semaphore_wait(barrier, NE - 1 + 2)
    over_peers(lambda o: a2a(0, o).start())
    own(0).start()

    spread = dot(expand, high) + dot(expand, mid) + dot(expand, low)
    weight = jnp.where(match, spread, 0.0)
    sgate[...] = jnp.sum(weight, axis=1, keepdims=True)
    weight_t = weight.T
    weight_high = weight_t.astype(BF16)
    comb[0] = weight_high
    comb[1] = (weight_t - weight_high.astype(F32)).astype(BF16)
    comb[2] = ones.T.astype(BF16)

    loads[4].wait()
    for g in range(NG):
        picked, gate = pick[g * GR : (g + 1) * GR, :], sgate[g * GR : (g + 1) * GR, :]
        blocks = [
            (dot(picked, cot[:, pl.ds(pl.multiple_of(c * DC, DC), DC)]) * gate).astype(BF16) for c in chunks
        ]
        for p in range(2 * NP):
            q = p + p // NP
            both = jnp.concatenate([blocks[q], blocks[q + 1]], axis=0)
            packed = dot(to_piece[p % NP], both).astype(BF16)
            c_send[g * GROUP : (g + 1) * GROUP, p] = packed.reshape(GROUP, PIECE, DC)
    own_cot.start()

    def next_cot(o):
        a2a(0, o).wait_send()
        a2a_cot(0, o).start()

    over_peers(next_cot)
    over_peers(lambda o: a2a_cot(1, o).start())

    for load in loads[5:]:
        load.wait()
    over_peers(lambda o: a2a(0, o).wait_recv())
    own(0).wait()
    unshuffle_all(0)
    over_peers(lambda o: a2a_cot(2, o).start())

    def put_hidden(m, n, value):
        for at in range(n * TILE, (n + 1) * TILE, 128):
            d, col = at // HALF, at % HALF
            hid[m, d, :, col : col + 128] = value[:, at - n * TILE : at - n * TILE + 128]

    for n in range(FF // TILE):
        cols = slice(n * TILE, (n + 1) * TILE)
        gate_pre = dot(x_rows[...], wg[:, cols])
        up_pre = dot(x_rows[...], wu[:, cols])
        sig = 1.0 / (1.0 + jnp.exp(-gate_pre))
        silu = gate_pre * sig
        fac[0, :, cols] = silu
        fac[1, :, cols] = up_pre * sig * (1.0 + gate_pre * (1.0 - sig))
        put_hidden(0, n, (silu * up_pre).astype(BF16))

    def take_cot(q):
        at = pl.ds(pl.multiple_of(chunks[q] * DC, DC), DC)
        base, i = NP * (q // NQ), q % NQ
        for g in range(NG):
            def piece(p):
                return c_recv[g * GROUP : (g + 1) * GROUP, p].reshape(GROUP * PIECE, DC)

            total = None
            if i < NP:
                total = dot(from_piece[i, :GR, :], piece(base + i))
            if i > 0:
                more = dot(from_piece[i - 1, GR:, :], piece(base + i - 1))
                total = more if total is None else total + more
            c_rows[g * GR : (g + 1) * GR, at] = total.astype(BF16)
        lt[0, chunks[q]] = c_rows[:, at].T

    def part(m, h, c):
        return dot(lt[(m + 1) // 2, c], hid[m, h])

    def chunk(d, i):
        return (z + (1 - 2 * d) * (4 - (i + 1) // 2) + ND) % ND

    def first(m, d, i):
        rs_send[m, d, i] = part(m, (d + i) % 2, chunk(d, i)).astype(BF16)
        link(m, d, i).start()

    def then(m, d, i):
        mine = part(m, (d + i) % 2, chunk(d, i))
        link(m, d, i - 2).wait_recv()
        rs_send[m, d, i] = (mine + rs_recv[m, d, i - 2].astype(F32)).astype(BF16)
        link(m, d, i).start()

    def begin(lowest, count, i):
        def body(j, _):
            first(lowest + j // 2, j % 2, i)
            return 0

        lax.fori_loop(0, 2 * count, body, 0)

    def both_ways(m, i):
        def body(d, _):
            then(m, d, i)
            return 0

        lax.fori_loop(0, 2, body, 0)

    def rounds(start, end):
        def body(j, _):
            m = (j // 2) % 3
            then(m, j % 2, 2 + j // 6 + 2 * ((2 - m) // 2))
            return 0

        lax.fori_loop(6 * start, 6 * end, body, 0)

    def late_rounds(start, end):
        def body(j, _):
            then(1 + (j // 2) % 2, j % 2, 2 + j // 4)
            return 0

        lax.fori_loop(4 * start, 4 * end, body, 0)

    over_peers(lambda o: a2a_cot(0, o).wait_recv())
    own_cot.wait()
    take_cot(0)
    begin(0, 1, 0)

    def whole(m):
        return jnp.concatenate([hid[m, 0], hid[m, 1]], axis=1)

    def stack_rows(q, rows):
        for g in range(NG):
            stack[g, q] = rows[g * GR : (g + 1) * GR].astype(BF16)

    for q in range(NQ):
        stack_rows(q, dot_t(whole(0), wd[q * QW : (q + 1) * QW, :]))
    for g in range(NG):
        shuffle_out(1, g, lambda q: stack[g, q])

    for j in range(ND):
        lt[1, j] = x_rows[:, j * DC : (j + 1) * DC].T
    over_peers(lambda o: a2a_cot(1, o).wait_recv())
    for q in (1, 2):
        take_cot(q)
    begin(0, 1, 1)
    take_cot(3)
    both_ways(0, 2)
    over_peers(lambda o: a2a_cot(2, o).wait_recv())
    for q in (4, 5, 6, 7):
        take_cot(q)
    over_peers(lambda o: a2a(1, o).start())
    own(1).start()
    both_ways(0, 3)

    for n in range(FF // TILE):
        cols = slice(n * TILE, (n + 1) * TILE)
        back = dot(c_rows[...], wd[:, cols])
        put_hidden(2, n, (back * fac[0, :, cols]).astype(BF16))
        put_hidden(1, n, (back * fac[1, :, cols]).astype(BF16))
    begin(1, 2, 0)
    begin(1, 2, 1)

    for q in range(NQ):
        rows = slice(q * QW, (q + 1) * QW)
        stack_rows(q, dot_t(whole(1), wg[rows, :]) + dot_t(whole(2), wu[rows, :]))
    for g in range(NG):
        shuffle_out(2, g, lambda q: stack[g, q])
    over_peers(lambda o: a2a(2, o).start())
    own(2).start()

    rounds(0, 2)
    over_peers(lambda o: a2a(1, o).wait_recv())
    own(1).wait()
    unshuffle_all(1)
    for q in range(NQ):
        cols = slice(q * QW, (q + 1) * QW)
        lo_ref[:, cols] = (dot(comb[0], x_rows[:, cols]) + dot(comb[1], x_rows[:, cols])).astype(BF16)

    rounds(2, 3)
    over_peers(lambda o: a2a(2, o).wait_recv())
    own(2).wait()
    unshuffle_all(2)
    for q in range(NQ):
        cols = slice(q * QW, (q + 1) * QW)
        gi_ref[:, cols] = dot(comb[2], x_rows[:, cols]).astype(BF16)

    def finish(m, out):
        for h in range(2):
            mine = part(m, h, z)
            link(m, 1 - h, LINKS - 2).wait_recv()
            mine = mine + rs_recv[m, 1 - h, LINKS - 2].astype(F32)
            link(m, h, LINKS - 1).wait_recv()
            total = mine + rs_recv[m, h, LINKS - 1].astype(F32)
            out[:, h * HALF : (h + 1) * HALF] = total.astype(BF16)

    late_rounds(3, 4)
    finish(0, gd_ref)
    late_rounds(4, 5)
    for p in (1, 2):
        over_peers(lambda o: a2a(p, o).wait_send())
    for t in range(len(STAGES)):
        over_peers(lambda o: a2a_cot(t, o).wait_send())
    finish(1, gg_ref)
    finish(2, gu_ref)

    def drain(i, _):
        link((i // 2) % 3, i % 2, i // 6).wait_send()
        return 0

    lax.fori_loop(0, 6 * LINKS, drain, 0)


def place(*refs):
    ins, outs, sem = refs[:5], refs[5:10], refs[10]
    stores = [
        pltpu.make_async_copy(ins[i], outs[i] if i < 2 else outs[i].at[0], sem.at[i]) for i in range(5)
    ]
    for store in stores:
        store.start()
    for store in stores:
        store.wait()


def shards(activations, expert_ids, route_gates, gate_proj, up_proj, down_proj, cotangent):
    vmem = pl.BlockSpec(memory_space=pltpu.VMEM)
    anywhere = pl.BlockSpec(memory_space=pl.ANY)
    dma = pltpu.SemaphoreType.DMA
    tokens = jax.ShapeDtypeStruct((TOK, D), BF16)
    grads = jax.ShapeDtypeStruct((DC, FF), BF16)
    out = pl.pallas_call(
        kernel,
        out_shape=tuple(pltpu.VMEM(s.shape, BF16) for s in (tokens,) * 2 + (grads,) * 3),
        in_specs=[anywhere] * 9,
        out_specs=(vmem,) * 5,
        scratch_shapes=[
            pltpu.VMEM((TOP, TOK), jnp.int32),
            pltpu.VMEM((TOP, TOK), F32),
            pltpu.VMEM((TOK, D), BF16),
            pltpu.VMEM((TOK, D), BF16),
            pltpu.VMEM((D, FF), BF16),
            pltpu.VMEM((D, FF), BF16),
            pltpu.VMEM((D, FF), BF16),
            pltpu.VMEM((NP, GROUP * PIECE, 2 * GR), BF16),
            pltpu.VMEM((NP, 2 * GR, GROUP * PIECE), BF16),
            pltpu.VMEM((SLOTS, TOK), BF16),
            pltpu.VMEM((SLOTS, 1), F32),
            pltpu.VMEM((3, TOK, SLOTS), BF16),
            pltpu.VMEM((3, NE, NP, PIECE, QW), BF16),
            pltpu.VMEM((3, NE, NP, PIECE, QW), BF16),
            pltpu.VMEM((NE, 2 * NP, PIECE, DC), BF16),
            pltpu.VMEM((NE, 2 * NP, PIECE, DC), BF16),
            pltpu.VMEM((NG, NQ, GR, QW), BF16),
            pltpu.VMEM((SLOTS, D), BF16),
            pltpu.VMEM((SLOTS, D), BF16),
            pltpu.VMEM((2, ND, DC, SLOTS), BF16),
            pltpu.VMEM((2, SLOTS, FF), F32),
            pltpu.VMEM((3, 2, SLOTS, HALF), BF16),
            pltpu.VMEM((3, 2, LINKS, DC, HALF), BF16),
            pltpu.VMEM((3, 2, LINKS, DC, HALF), BF16),
            dma((9,)),
            dma((4,)),
            dma((3, NE)),
            dma((3, NE)),
            dma((len(STAGES), NE)),
            dma((len(STAGES), NE)),
            dma((3, 2, LINKS)),
            dma((3, 2, LINKS)),
        ],
        compiler_params=pltpu.CompilerParams(
            collective_id=0, has_side_effects=True, vmem_limit_bytes=54 * 2**20
        ),
        cost_estimate=pl.CostEstimate(flops=12 * 10**9, bytes_accessed=15 * 10**6, transcendentals=300000),
        name="expert_layer",
    )(expert_ids.T, route_gates.T, activations, cotangent, gate_proj, up_proj, down_proj, *constants())
    kept = jax.ShapeDtypeStruct((1, DC, FF), BF16)
    return pl.pallas_call(
        place,
        out_shape=(tokens,) * 2 + (kept,) * 3,
        in_specs=[vmem] * 5,
        out_specs=(anywhere,) * 5,
        scratch_shapes=[dma((5,))],
        compiler_params=pltpu.CompilerParams(vmem_limit_bytes=2**20),
        name="place",
    )(*out)


def solution(mesh):
    in_specs = (
        P(("dp", "expert"), None),
        P(("dp", "expert"), None),
        P(("dp", "expert"), None),
        P("expert", None, None),
        P("expert", None, None),
        P("expert", None, None),
        P(("dp", "expert"), None),
    )
    out_specs = (
        P(("dp", "expert"), None),
        P(("dp", "expert"), None),
        P("expert", "dp", None),
        P("expert", "dp", None),
        P("expert", "dp", None),
    )
    return jax.shard_map(shards, mesh=mesh, in_specs=in_specs, out_specs=out_specs, check_vma=False)
```

```python
import functools

import jax
import jax.numpy as jnp
import numpy as np
from jax import lax
from jax.experimental import pallas as pl
from jax.experimental.pallas import tpu as pltpu
from jax.sharding import PartitionSpec as P

MESH = pl.DeviceIdType.MESH
BF16 = jnp.bfloat16
F32 = jnp.float32

CAP = 12
NE = 32
ND = 8
TOK = 128
TOP = 8
D = 2048
FF = 768
SLOTS = NE * CAP
GROUP = 8
NG = NE // GROUP
NQ = 4
QW = D // NQ
GR = GROUP * CAP
PIECE = 16
NP = CAP * NQ // PIECE
FIRST = 20
STAGES = ((0, 1), (1, 3), (3, 6))
OFFSETS = (4, 3, -3, 2, -2, 1, -1, 0)
LINKS = ND - 1
DC = D // ND
HALF = FF // 2
TILE = 256


def dot(a, b):
    return jnp.dot(a, b, preferred_element_type=F32)


def dot_t(a, b):
    return lax.dot_general(a, b, (((1,), (1,)), ((), ())), preferred_element_type=F32)


def constants():
    table = np.zeros((NP, GROUP * PIECE, 2 * GR), np.float32)
    for p in range(NP):
        for s in range(GROUP):
            for u in range(PIECE):
                q, r = divmod(p * PIECE + u, CAP)
                table[p, s * PIECE + u, (q - p) * GR + s * CAP + r] = 1.0
    return jnp.asarray(table, BF16), jnp.asarray(table.transpose(0, 2, 1), BF16)


def kernel(
    ids_hbm, gates_hbm, act_hbm, cot_hbm, wg_hbm, wu_hbm, wd_hbm, to_hbm, from_hbm,
    lo_ref, gi_ref, gg_ref, gu_ref, gd_ref,
    ids_ref, gates_ref, act, cot, wg, wu, wd, to_piece, from_piece, pick, sgate, comb, send, recv, c_send, c_recv, stack, x_rows, c_rows,
    lt, fac, hid, rs_send, rs_recv,
    wsem, lsem, ssem, rsem, csem, crem, zs, zr,
):
    me = lax.axis_index("expert")
    z = lax.axis_index("dp")
    my_y, my_x, my_c = me // 8, (me // 2) % 4, me % 2

    def peer(o):
        return (((my_y + o // 8) % 4) * 4 + (my_x + (o // 2) % 4) % 4) * 2 + (my_c + o % 2) % 2

    sources = (
        (ids_hbm, ids_ref), (gates_hbm, gates_ref), (act_hbm, act), (to_hbm, to_piece), (cot_hbm, cot),
        (from_hbm, from_piece), (wg_hbm.at[0], wg), (wu_hbm.at[0], wu), (wd_hbm.at[0], wd),
    )
    loads = [pltpu.make_async_copy(a, b, wsem.at[i]) for i, (a, b) in enumerate(sources)]
    for load in loads[:4]:
        load.start()

    barrier = pltpu.get_barrier_semaphore()

    def greet(o, _):
        pl.semaphore_signal(barrier, inc=1, device_id={"expert": peer(o)}, device_id_type=MESH)
        return 0

    lax.fori_loop(1, NE, greet, 0)
    for step in (1, ND - 1):
        pl.semaphore_signal(barrier, inc=1, device_id={"dp": (z + step) % ND}, device_id_type=MESH)
    for load in loads[4:]:
        load.start()

    def far_peers(f):
        def body(i, _):
            f(i + FIRST)
            return 0

        lax.fori_loop(0, NE - FIRST, body, 0)

    def near_peers(f):
        def body(i, _):
            f(i)
            return 0

        lax.fori_loop(1, FIRST, body, 0)

    def over_peers(f):
        far_peers(f)
        near_peers(f)

    def exchange(p, to, source, held, ssem):
        return pltpu.make_async_remote_copy(
            src_ref=send.at[p, source],
            dst_ref=recv.at[p, held],
            send_sem=ssem,
            recv_sem=rsem.at[p],
            device_id={"expert": to},
            device_id_type=MESH,
        )

    def a2a(p, o, group=0):
        to = peer(o)
        return exchange(p, to, to, me, ssem.at[p, group])

    def all_of(p, count=NE - 1, group=0):
        some = pl.ds(0, count)
        return exchange(p, peer(1), some, some, ssem.at[p, group])

    def cot_blocks(t, to, source, held):
        start, end = STAGES[t]
        pieces = pl.ds(start, end - start)
        return pltpu.make_async_remote_copy(
            src_ref=c_send.at[source, pieces],
            dst_ref=c_recv.at[held, pieces],
            send_sem=csem.at[t],
            recv_sem=crem.at[t],
            device_id={"expert": to},
            device_id_type=MESH,
        )

    def a2a_cot(t, o):
        to = peer(o)
        return cot_blocks(t, to, to, me)

    def all_of_cot(t):
        some = pl.ds(0, NE - 1)
        return cot_blocks(t, peer(1), some, some)

    def own(p):
        return pltpu.make_async_copy(send.at[p, me], recv.at[p, me], lsem.at[p])

    own_cot = pltpu.make_async_copy(c_send.at[me], c_recv.at[me], lsem.at[3])

    def links(source, held, sem, d):
        return pltpu.make_async_remote_copy(
            src_ref=source,
            dst_ref=held,
            send_sem=zs,
            recv_sem=sem,
            device_id={"dp": (z + 1 - 2 * d + ND) % ND},
            device_id_type=MESH,
        )

    def link(m, d, i):
        return links(rs_send.at[m, d, i], rs_recv.at[m, d, i], zr.at[m, d, i], d)

    chunks = [(z + off + ND) % ND for off in OFFSETS]

    loads[0].wait()
    loads[1].wait()
    ids = ids_ref[...]
    gates = gates_ref[...]
    experts = lax.broadcasted_iota(jnp.int32, (NE, TOK), 0)
    named = jnp.zeros((NE, TOK), F32)
    gate_of = jnp.zeros((NE, TOK), F32)
    for k in range(TOP):
        hit = ids[k : k + 1, :] == experts
        named = named + jnp.where(hit, 1.0, 0.0)
        gate_of = gate_of + jnp.where(hit, gates[k : k + 1, :], 0.0)
    before = lax.broadcasted_iota(jnp.int32, (TOK, TOK), 0) < lax.broadcasted_iota(jnp.int32, (TOK, TOK), 1)
    earlier = dot(named.astype(BF16), jnp.where(before, 1.0, 0.0).astype(BF16))
    slot_of = jnp.where(named > 0.0, earlier, -1.0).astype(BF16)
    slots = lax.broadcasted_iota(jnp.int32, (SLOTS, NE), 0)
    first_slot = lax.broadcasted_iota(jnp.int32, (SLOTS, NE), 1) * CAP
    expand = jnp.where((slots >= first_slot) & (slots < first_slot + CAP), 1.0, 0.0)
    row = jnp.sum(expand * (slots - first_slot).astype(F32), axis=1, keepdims=True)
    expand = expand.astype(BF16)
    match = dot(expand, slot_of) == row
    high = gate_of.astype(BF16)
    rest = gate_of - high.astype(F32)
    mid = rest.astype(BF16)
    low = (rest - mid.astype(F32)).astype(BF16)
    ones = jnp.where(match, 1.0, 0.0)
    pick[...] = ones.astype(BF16)

    def shuffle_out(p, g, block):
        for t in range(NP):
            both = jnp.concatenate([block(t), block(t + 1)], axis=0)
            packed = dot(to_piece[t], both).astype(BF16)
            send[p, g * GROUP : (g + 1) * GROUP, t] = packed.reshape(GROUP, PIECE, QW)

    def unshuffle(p, q):
        out = []
        for g in range(NG):
            def piece(t):
                return recv[p, g * GROUP : (g + 1) * GROUP, t].reshape(GROUP * PIECE, QW)

            total = None
            if q < NP:
                total = dot(from_piece[q, :GR, :], piece(q))
            if q > 0:
                more = dot(from_piece[q - 1, GR:, :], piece(q - 1))
                total = more if total is None else total + more
            out.append(total.astype(BF16))
        return out

    def unshuffle_all(p):
        for q in range(NQ):
            for g, rows in enumerate(unshuffle(p, q)):
                x_rows[g * GR : (g + 1) * GR, q * QW : (q + 1) * QW] = rows

    loads[2].wait()
    loads[3].wait()
    for g in range(NG):
        rows = dot(pick[g * GR : (g + 1) * GR, :], act[...]).astype(BF16)
        shuffle_out(0, g, lambda q: rows[:, q * QW : (q + 1) * QW])
    pl.semaphore_wait(barrier, NE - 1 + 2)
    far_peers(lambda o: a2a(0, o, 0).start())
    near_peers(lambda o: a2a(0, o, 1).start())
    own(0).start()

    spread = dot(expand, high) + dot(expand, mid) + dot(expand, low)
    weight = jnp.where(match, spread, 0.0)
    sgate[...] = jnp.sum(weight, axis=1, keepdims=True)
    weight_t = weight.T
    weight_high = weight_t.astype(BF16)
    comb[0] = weight_high
    comb[1] = (weight_t - weight_high.astype(F32)).astype(BF16)
    comb[2] = ones.T.astype(BF16)

    loads[4].wait()
    for g in range(NG):
        picked, gate = pick[g * GR : (g + 1) * GR, :], sgate[g * GR : (g + 1) * GR, :]
        blocks = [
            (dot(picked, cot[:, pl.ds(pl.multiple_of(c * DC, DC), DC)]) * gate).astype(BF16) for c in chunks
        ]
        for p in range(2 * NP):
            q = p + p // NP
            both = jnp.concatenate([blocks[q], blocks[q + 1]], axis=0)
            packed = dot(to_piece[p % NP], both).astype(BF16)
            c_send[g * GROUP : (g + 1) * GROUP, p] = packed.reshape(GROUP, PIECE, DC)
    own_cot.start()

    all_of(0, NE - FIRST, 0).wait_send()
    far_peers(lambda o: a2a_cot(0, o).start())
    all_of(0, FIRST - 1, 1).wait_send()
    near_peers(lambda o: a2a_cot(0, o).start())
    over_peers(lambda o: a2a_cot(1, o).start())

    for load in loads[5:]:
        load.wait()
    all_of(0).wait_recv()
    own(0).wait()
    unshuffle_all(0)
    over_peers(lambda o: a2a_cot(2, o).start())

    def put_hidden(m, n, value):
        for at in range(n * TILE, (n + 1) * TILE, 128):
            d, col = at // HALF, at % HALF
            hid[m, d, :, col : col + 128] = value[:, at - n * TILE : at - n * TILE + 128]

    for n in range(FF // TILE):
        cols = slice(n * TILE, (n + 1) * TILE)
        gate_pre = dot(x_rows[...], wg[:, cols])
        up_pre = dot(x_rows[...], wu[:, cols])
        sig = 1.0 / (1.0 + jnp.exp(-gate_pre))
        silu = gate_pre * sig
        fac[0, :, cols] = silu
        fac[1, :, cols] = up_pre * sig * (1.0 + gate_pre * (1.0 - sig))
        put_hidden(0, n, (silu * up_pre).astype(BF16))

    def take_cot(q):
        at = pl.ds(pl.multiple_of(chunks[q] * DC, DC), DC)
        base, i = NP * (q // NQ), q % NQ
        for g in range(NG):
            def piece(p):
                return c_recv[g * GROUP : (g + 1) * GROUP, p].reshape(GROUP * PIECE, DC)

            total = None
            if i < NP:
                total = dot(from_piece[i, :GR, :], piece(base + i))
            if i > 0:
                more = dot(from_piece[i - 1, GR:, :], piece(base + i - 1))
                total = more if total is None else total + more
            c_rows[g * GR : (g + 1) * GR, at] = total.astype(BF16)
        lt[0, chunks[q]] = c_rows[:, at].T

    def part(m, h, c):
        return dot(lt[(m + 1) // 2, c], hid[m, h])

    def chunk(d, i):
        return (z + (1 - 2 * d) * (4 - (i + 1) // 2) + ND) % ND

    def first(m, d, i):
        rs_send[m, d, i] = part(m, (d + i) % 2, chunk(d, i)).astype(BF16)
        link(m, d, i).start()

    def then(m, d, i):
        mine = part(m, (d + i) % 2, chunk(d, i))
        link(m, d, i - 2).wait_recv()
        rs_send[m, d, i] = (mine + rs_recv[m, d, i - 2].astype(F32)).astype(BF16)
        link(m, d, i).start()

    def begin(lowest, count, i):
        def body(j, _):
            first(lowest + j // 2, j % 2, i)
            return 0

        lax.fori_loop(0, 2 * count, body, 0)

    def both_ways(m, i):
        def body(d, _):
            then(m, d, i)
            return 0

        lax.fori_loop(0, 2, body, 0)

    def rounds(start, end):
        def body(j, _):
            m = (j // 2) % 3
            then(m, j % 2, 2 + j // 6 + 2 * ((2 - m) // 2))
            return 0

        lax.fori_loop(6 * start, 6 * end, body, 0)

    def late_rounds(start, end):
        def body(j, _):
            then(1 + (j // 2) % 2, j % 2, 2 + j // 4)
            return 0

        lax.fori_loop(4 * start, 4 * end, body, 0)

    all_of_cot(0).wait_recv()
    own_cot.wait()
    take_cot(0)
    begin(0, 1, 0)

    def whole(m):
        return jnp.concatenate([hid[m, 0], hid[m, 1]], axis=1)

    def stack_rows(q, rows):
        for g in range(NG):
            stack[g, q] = rows[g * GR : (g + 1) * GR].astype(BF16)

    for q in range(NQ):
        stack_rows(q, dot_t(whole(0), wd[q * QW : (q + 1) * QW, :]))
    for g in range(NG):
        shuffle_out(1, g, lambda q: stack[g, q])

    for j in range(ND):
        lt[1, j] = x_rows[:, j * DC : (j + 1) * DC].T
    all_of_cot(1).wait_recv()
    for q in (1, 2):
        take_cot(q)
    begin(0, 1, 1)
    take_cot(3)
    both_ways(0, 2)
    all_of_cot(2).wait_recv()
    for q in (4, 5, 6, 7):
        take_cot(q)
    over_peers(lambda o: a2a(1, o).start())
    own(1).start()
    both_ways(0, 3)

    for n in range(FF // TILE):
        cols = slice(n * TILE, (n + 1) * TILE)
        back = dot(c_rows[...], wd[:, cols])
        put_hidden(2, n, (back * fac[0, :, cols]).astype(BF16))
        put_hidden(1, n, (back * fac[1, :, cols]).astype(BF16))
    begin(1, 2, 0)
    begin(1, 2, 1)

    for q in range(NQ):
        rows = slice(q * QW, (q + 1) * QW)
        stack_rows(q, dot_t(whole(1), wg[rows, :]) + dot_t(whole(2), wu[rows, :]))
    for g in range(NG):
        shuffle_out(2, g, lambda q: stack[g, q])
    over_peers(lambda o: a2a(2, o).start())
    own(2).start()

    rounds(0, 2)
    all_of(1).wait_recv()
    own(1).wait()
    unshuffle_all(1)
    for q in range(NQ):
        cols = slice(q * QW, (q + 1) * QW)
        lo_ref[:, cols] = (dot(comb[0], x_rows[:, cols]) + dot(comb[1], x_rows[:, cols])).astype(BF16)

    rounds(2, 3)
    all_of(2).wait_recv()
    own(2).wait()
    unshuffle_all(2)
    for q in range(NQ):
        cols = slice(q * QW, (q + 1) * QW)
        gi_ref[:, cols] = dot(comb[2], x_rows[:, cols]).astype(BF16)

    def finish(m, out):
        for h in range(2):
            mine = part(m, h, z)
            link(m, 1 - h, LINKS - 2).wait_recv()
            mine = mine + rs_recv[m, 1 - h, LINKS - 2].astype(F32)
            link(m, h, LINKS - 1).wait_recv()
            total = mine + rs_recv[m, h, LINKS - 1].astype(F32)
            out[:, h * HALF : (h + 1) * HALF] = total.astype(BF16)

    late_rounds(3, 4)
    finish(0, gd_ref)
    late_rounds(4, 5)
    for p in (1, 2):
        all_of(p).wait_send()
    for t in range(len(STAGES)):
        all_of_cot(t).wait_send()
    finish(1, gg_ref)
    finish(2, gu_ref)

    links(rs_send, rs_recv, zr.at[0, 0, 0], 0).wait_send()


def place(*refs):
    ins, outs, sem = refs[:5], refs[5:10], refs[10]
    stores = [
        pltpu.make_async_copy(ins[i], outs[i] if i < 2 else outs[i].at[0], sem.at[i]) for i in range(5)
    ]
    for store in stores:
        store.start()
    for store in stores:
        store.wait()


def shards(activations, expert_ids, route_gates, gate_proj, up_proj, down_proj, cotangent):
    vmem = pl.BlockSpec(memory_space=pltpu.VMEM)
    anywhere = pl.BlockSpec(memory_space=pl.ANY)
    dma = pltpu.SemaphoreType.DMA
    tokens = jax.ShapeDtypeStruct((TOK, D), BF16)
    grads = jax.ShapeDtypeStruct((DC, FF), BF16)
    out = pl.pallas_call(
        kernel,
        out_shape=tuple(pltpu.VMEM(s.shape, BF16) for s in (tokens,) * 2 + (grads,) * 3),
        in_specs=[anywhere] * 9,
        out_specs=(vmem,) * 5,
        scratch_shapes=[
            pltpu.VMEM((TOP, TOK), jnp.int32),
            pltpu.VMEM((TOP, TOK), F32),
            pltpu.VMEM((TOK, D), BF16),
            pltpu.VMEM((TOK, D), BF16),
            pltpu.VMEM((D, FF), BF16),
            pltpu.VMEM((D, FF), BF16),
            pltpu.VMEM((D, FF), BF16),
            pltpu.VMEM((NP, GROUP * PIECE, 2 * GR), BF16),
            pltpu.VMEM((NP, 2 * GR, GROUP * PIECE), BF16),
            pltpu.VMEM((SLOTS, TOK), BF16),
            pltpu.VMEM((SLOTS, 1), F32),
            pltpu.VMEM((3, TOK, SLOTS), BF16),
            pltpu.VMEM((3, NE, NP, PIECE, QW), BF16),
            pltpu.VMEM((3, NE, NP, PIECE, QW), BF16),
            pltpu.VMEM((NE, 2 * NP, PIECE, DC), BF16),
            pltpu.VMEM((NE, 2 * NP, PIECE, DC), BF16),
            pltpu.VMEM((NG, NQ, GR, QW), BF16),
            pltpu.VMEM((SLOTS, D), BF16),
            pltpu.VMEM((SLOTS, D), BF16),
            pltpu.VMEM((2, ND, DC, SLOTS), BF16),
            pltpu.VMEM((2, SLOTS, FF), F32),
            pltpu.VMEM((3, 2, SLOTS, HALF), BF16),
            pltpu.VMEM((3, 2, LINKS, DC, HALF), BF16),
            pltpu.VMEM((3, 2, LINKS, DC, HALF), BF16),
            dma((9,)),
            dma((4,)),
            dma((3, 2)),
            dma((3,)),
            dma((len(STAGES),)),
            dma((len(STAGES),)),
            dma,
            dma((3, 2, LINKS)),
        ],
        compiler_params=pltpu.CompilerParams(
            collective_id=0, has_side_effects=True, vmem_limit_bytes=54 * 2**20
        ),
        cost_estimate=pl.CostEstimate(flops=12 * 10**9, bytes_accessed=15 * 10**6, transcendentals=300000),
        name="expert_layer",
    )(expert_ids.T, route_gates.T, activations, cotangent, gate_proj, up_proj, down_proj, *constants())
    kept = jax.ShapeDtypeStruct((1, DC, FF), BF16)
    return pl.pallas_call(
        place,
        out_shape=(tokens,) * 2 + (kept,) * 3,
        in_specs=[vmem] * 5,
        out_specs=(anywhere,) * 5,
        scratch_shapes=[dma((5,))],
        compiler_params=pltpu.CompilerParams(vmem_limit_bytes=2**20),
        name="place",
    )(*out)


def solution(mesh):
    in_specs = (
        P(("dp", "expert"), None),
        P(("dp", "expert"), None),
        P(("dp", "expert"), None),
        P("expert", None, None),
        P("expert", None, None),
        P("expert", None, None),
        P(("dp", "expert"), None),
    )
    out_specs = (
        P(("dp", "expert"), None),
        P(("dp", "expert"), None),
        P("expert", "dp", None),
        P("expert", "dp", None),
        P("expert", "dp", None),
    )
    return jax.shard_map(shards, mesh=mesh, in_specs=in_specs, out_specs=out_specs, check_vma=False)
```

```python
import functools

import jax
import jax.numpy as jnp
import numpy as np
from jax import lax
from jax.experimental import pallas as pl
from jax.experimental.pallas import tpu as pltpu
from jax.sharding import PartitionSpec as P

MESH = pl.DeviceIdType.MESH
BF16 = jnp.bfloat16
F32 = jnp.float32

CAP = 12
NE = 32
ND = 8
TOK = 128
TOP = 8
D = 2048
FF = 768
SLOTS = NE * CAP
GROUP = 8
NG = NE // GROUP
NQ = 4
QW = D // NQ
GR = GROUP * CAP
PIECE = 16
NP = CAP * NQ // PIECE
ORDER = sorted(range(1, NE), key=lambda o: (-abs(2 - abs(2 - o // 8)) - abs(2 - abs(2 - o // 2 % 4)), 2 - abs(2 - o // 8), o % 2, o))
STAGES = ((0, 1), (1, 3), (3, 6))
OFFSETS = (4, 3, -3, 2, -2, 1, -1, 0)
LINKS = ND - 1
DC = D // ND
HALF = FF // 2
TILE = 256


def dot(a, b):
    return jnp.dot(a, b, preferred_element_type=F32)


def dot_t(a, b):
    return lax.dot_general(a, b, (((1,), (1,)), ((), ())), preferred_element_type=F32)


def constants():
    table = np.zeros((NP, GROUP * PIECE, 2 * GR), np.float32)
    for p in range(NP):
        for s in range(GROUP):
            for u in range(PIECE):
                q, r = divmod(p * PIECE + u, CAP)
                table[p, s * PIECE + u, (q - p) * GR + s * CAP + r] = 1.0
    return jnp.asarray(table, BF16), jnp.asarray(table.transpose(0, 2, 1), BF16)


def kernel(
    ids_hbm, gates_hbm, act_hbm, cot_hbm, wg_hbm, wu_hbm, wd_hbm, to_hbm, from_hbm,
    lo_ref, gi_ref, gg_ref, gu_ref, gd_ref,
    ids_ref, gates_ref, act, cot, wg, wu, wd, to_piece, from_piece, pick, sgate, comb, send, recv, c_send, c_recv, stack, x_rows, c_rows,
    lt, fac, hid, rs_send, rs_recv,
    wsem, lsem, ssem, rsem, csem, crem, zs, zr,
):
    me = lax.axis_index("expert")
    z = lax.axis_index("dp")
    my_y, my_x, my_c = me // 8, (me // 2) % 4, me % 2

    def peer(o):
        return (((my_y + o // 8) % 4) * 4 + (my_x + (o // 2) % 4) % 4) * 2 + (my_c + o % 2) % 2

    sources = (
        (ids_hbm, ids_ref), (gates_hbm, gates_ref), (act_hbm, act), (to_hbm, to_piece), (cot_hbm, cot),
        (from_hbm, from_piece), (wg_hbm.at[0], wg), (wu_hbm.at[0], wu), (wd_hbm.at[0], wd),
    )
    loads = [pltpu.make_async_copy(a, b, wsem.at[i]) for i, (a, b) in enumerate(sources)]
    for load in loads[:4]:
        load.start()

    barrier = pltpu.get_barrier_semaphore()

    def greet(o, _):
        pl.semaphore_signal(barrier, inc=1, device_id={"expert": peer(o)}, device_id_type=MESH)
        return 0

    lax.fori_loop(1, NE, greet, 0)
    for step in (1, ND - 1):
        pl.semaphore_signal(barrier, inc=1, device_id={"dp": (z + step) % ND}, device_id_type=MESH)
    for load in loads[4:]:
        load.start()

    def over_peers(f):
        for n, o in enumerate(ORDER):
            f(n, o)

    def mirror(o):
        return ((4 - o // 8) % 4 * 4 + (4 - o // 2 % 4) % 4) * 2 + o % 2

    def exchange(p, to, source, held, sem):
        return pltpu.make_async_remote_copy(
            src_ref=send.at[p, source],
            dst_ref=recv.at[p, held],
            send_sem=ssem.at[p],
            recv_sem=rsem.at[sem],
            device_id={"expert": to},
            device_id_type=MESH,
        )

    def dispatch(n, o):
        to = peer(o)
        return exchange(0, to, to, n, n // GROUP)

    def arrived(g):
        count = GROUP if g < NG - 1 else GROUP - 1
        return exchange(0, peer(1), pl.ds(0, count), pl.ds(g * GROUP, count), g)

    def send_back(p, n, o):
        return exchange(p, peer(mirror(o)), n, me, NG - 1 + p)

    def all_of(p):
        some = pl.ds(0, NE - 1)
        return exchange(p, peer(1), some, some, NG - 1 + p)

    def cot_blocks(t, to, source, held):
        start, end = STAGES[t]
        pieces = pl.ds(start, end - start)
        return pltpu.make_async_remote_copy(
            src_ref=c_send.at[source, pieces],
            dst_ref=c_recv.at[held, pieces],
            send_sem=csem.at[t],
            recv_sem=crem.at[t],
            device_id={"expert": to},
            device_id_type=MESH,
        )

    def dispatch_cot(t, n, o):
        to = peer(o)
        return cot_blocks(t, to, to, n)

    def all_of_cot(t):
        some = pl.ds(0, NE - 1)
        return cot_blocks(t, peer(1), some, some)

    def own(p):
        source, held = (me, NE - 1) if p == 0 else (NE - 1, me)
        return pltpu.make_async_copy(send.at[p, source], recv.at[p, held], lsem.at[p])

    own_cot = pltpu.make_async_copy(c_send.at[me], c_recv.at[NE - 1], lsem.at[3])

    def links(source, held, sem, d):
        return pltpu.make_async_remote_copy(
            src_ref=source,
            dst_ref=held,
            send_sem=zs,
            recv_sem=sem,
            device_id={"dp": (z + 1 - 2 * d + ND) % ND},
            device_id_type=MESH,
        )

    def link(m, d, i):
        return links(rs_send.at[m, d, i], rs_recv.at[m, d, i], zr.at[m, d, i], d)

    chunks = [(z + off + ND) % ND for off in OFFSETS]

    loads[0].wait()
    loads[1].wait()
    ids = ids_ref[...]
    gates = gates_ref[...]
    experts = lax.broadcasted_iota(jnp.int32, (NE, TOK), 0)
    named = jnp.zeros((NE, TOK), F32)
    gate_of = jnp.zeros((NE, TOK), F32)
    for k in range(TOP):
        hit = ids[k : k + 1, :] == experts
        named = named + jnp.where(hit, 1.0, 0.0)
        gate_of = gate_of + jnp.where(hit, gates[k : k + 1, :], 0.0)
    before = lax.broadcasted_iota(jnp.int32, (TOK, TOK), 0) < lax.broadcasted_iota(jnp.int32, (TOK, TOK), 1)
    earlier = dot(named.astype(BF16), jnp.where(before, 1.0, 0.0).astype(BF16))
    slot_of = jnp.where(named > 0.0, earlier, -1.0).astype(BF16)
    slots = lax.broadcasted_iota(jnp.int32, (SLOTS, NE), 0)
    first_slot = lax.broadcasted_iota(jnp.int32, (SLOTS, NE), 1) * CAP
    expand = jnp.where((slots >= first_slot) & (slots < first_slot + CAP), 1.0, 0.0)
    row = jnp.sum(expand * (slots - first_slot).astype(F32), axis=1, keepdims=True)
    expand = expand.astype(BF16)
    match = dot(expand, slot_of) == row
    high = gate_of.astype(BF16)
    rest = gate_of - high.astype(F32)
    mid = rest.astype(BF16)
    low = (rest - mid.astype(F32)).astype(BF16)
    ones = jnp.where(match, 1.0, 0.0)
    pick[...] = ones.astype(BF16)

    def shuffle_out(p, g, block):
        for t in range(NP):
            both = jnp.concatenate([block(t), block(t + 1)], axis=0)
            packed = dot(to_piece[t], both).astype(BF16)
            send[p, g * GROUP : (g + 1) * GROUP, t] = packed.reshape(GROUP, PIECE, QW)

    def unshuffle(p, g):
        def piece(t):
            return recv[p, g * GROUP : (g + 1) * GROUP, t].reshape(GROUP * PIECE, QW)

        for q in range(NQ):
            total = None
            if q < NP:
                total = dot(from_piece[q, :GR, :], piece(q))
            if q > 0:
                more = dot(from_piece[q - 1, GR:, :], piece(q - 1))
                total = more if total is None else total + more
            x_rows[g * GR : (g + 1) * GR, q * QW : (q + 1) * QW] = total.astype(BF16)

    loads[2].wait()
    loads[3].wait()
    for g in range(NG):
        rows = dot(pick[g * GR : (g + 1) * GR, :], act[...]).astype(BF16)
        shuffle_out(0, g, lambda q: rows[:, q * QW : (q + 1) * QW])
    pl.semaphore_wait(barrier, NE - 1 + 2)
    over_peers(lambda n, o: dispatch(n, o).start())
    own(0).start()

    spread = dot(expand, high) + dot(expand, mid) + dot(expand, low)
    weight = jnp.where(match, spread, 0.0)
    sgate[...] = jnp.sum(weight, axis=1, keepdims=True)
    weight_t = weight.T
    weight_high = weight_t.astype(BF16)
    comb[0] = weight_high
    comb[1] = (weight_t - weight_high.astype(F32)).astype(BF16)
    comb[2] = ones.T.astype(BF16)

    loads[4].wait()
    for g in range(NG):
        picked, gate = pick[g * GR : (g + 1) * GR, :], sgate[g * GR : (g + 1) * GR, :]
        blocks = [
            (dot(picked, cot[:, pl.ds(pl.multiple_of(c * DC, DC), DC)]) * gate).astype(BF16) for c in chunks
        ]
        for p in range(2 * NP):
            q = p + p // NP
            both = jnp.concatenate([blocks[q], blocks[q + 1]], axis=0)
            packed = dot(to_piece[p % NP], both).astype(BF16)
            c_send[g * GROUP : (g + 1) * GROUP, p] = packed.reshape(GROUP, PIECE, DC)
    own_cot.start()

    for t in (0, 1):
        over_peers(lambda n, o: dispatch_cot(t, n, o).start())

    for load in loads[5:]:
        load.wait()
    def put_hidden(m, n, value, rows=slice(0, SLOTS)):
        for at in range(n * TILE, (n + 1) * TILE, 128):
            d, col = at // HALF, at % HALF
            hid[m, d, rows, col : col + 128] = value[:, at - n * TILE : at - n * TILE + 128]

    for half in range(2):
        for g in (2 * half, 2 * half + 1):
            arrived(g).wait_recv()
            if g == NG - 1:
                own(0).wait()
            unshuffle(0, g)
        if half == 1:
            over_peers(lambda n, o: dispatch_cot(2, n, o).start())
        rows = slice(half * SLOTS // 2, (half + 1) * SLOTS // 2)
        for n in range(FF // TILE):
            cols = slice(n * TILE, (n + 1) * TILE)
            gate_pre = dot(x_rows[rows, :], wg[:, cols])
            up_pre = dot(x_rows[rows, :], wu[:, cols])
            sig = 1.0 / (1.0 + jnp.exp(-gate_pre))
            silu = gate_pre * sig
            fac[0, rows, cols] = silu
            fac[1, rows, cols] = up_pre * sig * (1.0 + gate_pre * (1.0 - sig))
            put_hidden(0, n, (silu * up_pre).astype(BF16), rows)

    def take_cot(q):
        at = pl.ds(pl.multiple_of(chunks[q] * DC, DC), DC)
        base, i = NP * (q // NQ), q % NQ
        for g in range(NG):
            def piece(p):
                return c_recv[g * GROUP : (g + 1) * GROUP, p].reshape(GROUP * PIECE, DC)

            total = None
            if i < NP:
                total = dot(from_piece[i, :GR, :], piece(base + i))
            if i > 0:
                more = dot(from_piece[i - 1, GR:, :], piece(base + i - 1))
                total = more if total is None else total + more
            c_rows[g * GR : (g + 1) * GR, at] = total.astype(BF16)
        lt[0, chunks[q]] = c_rows[:, at].T

    def part(m, h, c):
        return dot(lt[(m + 1) // 2, c], hid[m, h])

    def chunk(d, i):
        return (z + (1 - 2 * d) * (4 - (i + 1) // 2) + ND) % ND

    def first(m, d, i):
        rs_send[m, d, i] = part(m, (d + i) % 2, chunk(d, i)).astype(BF16)
        link(m, d, i).start()

    def then(m, d, i):
        mine = part(m, (d + i) % 2, chunk(d, i))
        link(m, d, i - 2).wait_recv()
        rs_send[m, d, i] = (mine + rs_recv[m, d, i - 2].astype(F32)).astype(BF16)
        link(m, d, i).start()

    def begin(lowest, count, i):
        def body(j, _):
            first(lowest + j // 2, j % 2, i)
            return 0

        lax.fori_loop(0, 2 * count, body, 0)

    def both_ways(m, i):
        def body(d, _):
            then(m, d, i)
            return 0

        lax.fori_loop(0, 2, body, 0)

    def rounds(start, end):
        def body(j, _):
            m = (j // 2) % 3
            then(m, j % 2, 2 + j // 6 + 2 * ((2 - m) // 2))
            return 0

        lax.fori_loop(6 * start, 6 * end, body, 0)

    def late_rounds(start, end):
        def body(j, _):
            then(1 + (j // 2) % 2, j % 2, 2 + j // 4)
            return 0

        lax.fori_loop(4 * start, 4 * end, body, 0)

    all_of_cot(0).wait_recv()
    own_cot.wait()
    take_cot(0)
    begin(0, 1, 0)

    def whole(m):
        return jnp.concatenate([hid[m, 0], hid[m, 1]], axis=1)

    def stack_rows(q, rows):
        for g in range(NG):
            stack[g, q] = rows[g * GR : (g + 1) * GR].astype(BF16)

    for q in range(NQ):
        stack_rows(q, dot_t(whole(0), wd[q * QW : (q + 1) * QW, :]))
    for g in range(NG):
        shuffle_out(1, g, lambda q: stack[g, q])

    for j in range(ND):
        lt[1, j] = x_rows[:, j * DC : (j + 1) * DC].T
    all_of_cot(1).wait_recv()
    for q in (1, 2):
        take_cot(q)
    begin(0, 1, 1)
    take_cot(3)
    both_ways(0, 2)
    all_of_cot(2).wait_recv()
    for q in (4, 5, 6, 7):
        take_cot(q)
    over_peers(lambda n, o: send_back(1, n, o).start())
    own(1).start()
    both_ways(0, 3)

    for n in range(FF // TILE):
        cols = slice(n * TILE, (n + 1) * TILE)
        back = dot(c_rows[...], wd[:, cols])
        put_hidden(2, n, (back * fac[0, :, cols]).astype(BF16))
        put_hidden(1, n, (back * fac[1, :, cols]).astype(BF16))
    begin(1, 2, 0)
    begin(1, 2, 1)

    for q in range(NQ):
        rows = slice(q * QW, (q + 1) * QW)
        stack_rows(q, dot_t(whole(1), wg[rows, :]) + dot_t(whole(2), wu[rows, :]))
    for g in range(NG):
        shuffle_out(2, g, lambda q: stack[g, q])
    over_peers(lambda n, o: send_back(2, n, o).start())
    own(2).start()

    rounds(0, 2)
    all_of(1).wait_recv()
    own(1).wait()
    for g in range(NG):
        unshuffle(1, g)
    for q in range(NQ):
        cols = slice(q * QW, (q + 1) * QW)
        lo_ref[:, cols] = (dot(comb[0], x_rows[:, cols]) + dot(comb[1], x_rows[:, cols])).astype(BF16)

    rounds(2, 3)
    all_of(2).wait_recv()
    own(2).wait()
    for g in range(NG):
        unshuffle(2, g)
    for q in range(NQ):
        cols = slice(q * QW, (q + 1) * QW)
        gi_ref[:, cols] = dot(comb[2], x_rows[:, cols]).astype(BF16)

    def finish(m, out):
        for h in range(2):
            mine = part(m, h, z)
            link(m, 1 - h, LINKS - 2).wait_recv()
            mine = mine + rs_recv[m, 1 - h, LINKS - 2].astype(F32)
            link(m, h, LINKS - 1).wait_recv()
            total = mine + rs_recv[m, h, LINKS - 1].astype(F32)
            out[:, h * HALF : (h + 1) * HALF] = total.astype(BF16)

    late_rounds(3, 4)
    finish(0, gd_ref)
    late_rounds(4, 5)
    for p in range(3):
        all_of(p).wait_send()
    for t in range(len(STAGES)):
        all_of_cot(t).wait_send()
    finish(1, gg_ref)
    finish(2, gu_ref)

    links(rs_send, rs_recv, zr.at[0, 0, 0], 0).wait_send()


def place(*refs):
    ins, outs, sem = refs[:5], refs[5:10], refs[10]
    stores = [
        pltpu.make_async_copy(ins[i], outs[i] if i < 2 else outs[i].at[0], sem.at[i]) for i in range(5)
    ]
    for store in stores:
        store.start()
    for store in stores:
        store.wait()


def shards(activations, expert_ids, route_gates, gate_proj, up_proj, down_proj, cotangent):
    vmem = pl.BlockSpec(memory_space=pltpu.VMEM)
    anywhere = pl.BlockSpec(memory_space=pl.ANY)
    dma = pltpu.SemaphoreType.DMA
    tokens = jax.ShapeDtypeStruct((TOK, D), BF16)
    grads = jax.ShapeDtypeStruct((DC, FF), BF16)
    out = pl.pallas_call(
        kernel,
        out_shape=tuple(pltpu.VMEM(s.shape, BF16) for s in (tokens,) * 2 + (grads,) * 3),
        in_specs=[anywhere] * 9,
        out_specs=(vmem,) * 5,
        scratch_shapes=[
            pltpu.VMEM((TOP, TOK), jnp.int32),
            pltpu.VMEM((TOP, TOK), F32),
            pltpu.VMEM((TOK, D), BF16),
            pltpu.VMEM((TOK, D), BF16),
            pltpu.VMEM((D, FF), BF16),
            pltpu.VMEM((D, FF), BF16),
            pltpu.VMEM((D, FF), BF16),
            pltpu.VMEM((NP, GROUP * PIECE, 2 * GR), BF16),
            pltpu.VMEM((NP, 2 * GR, GROUP * PIECE), BF16),
            pltpu.VMEM((SLOTS, TOK), BF16),
            pltpu.VMEM((SLOTS, 1), F32),
            pltpu.VMEM((3, TOK, SLOTS), BF16),
            pltpu.VMEM((3, NE, NP, PIECE, QW), BF16),
            pltpu.VMEM((3, NE, NP, PIECE, QW), BF16),
            pltpu.VMEM((NE, 2 * NP, PIECE, DC), BF16),
            pltpu.VMEM((NE, 2 * NP, PIECE, DC), BF16),
            pltpu.VMEM((NG, NQ, GR, QW), BF16),
            pltpu.VMEM((SLOTS, D), BF16),
            pltpu.VMEM((SLOTS, D), BF16),
            pltpu.VMEM((2, ND, DC, SLOTS), BF16),
            pltpu.VMEM((2, SLOTS, FF), F32),
            pltpu.VMEM((3, 2, SLOTS, HALF), BF16),
            pltpu.VMEM((3, 2, LINKS, DC, HALF), BF16),
            pltpu.VMEM((3, 2, LINKS, DC, HALF), BF16),
            dma((9,)),
            dma((4,)),
            dma((3,)),
            dma((NG + 2,)),
            dma((len(STAGES),)),
            dma((len(STAGES),)),
            dma,
            dma((3, 2, LINKS)),
        ],
        compiler_params=pltpu.CompilerParams(
            collective_id=0, has_side_effects=True, vmem_limit_bytes=54 * 2**20
        ),
        cost_estimate=pl.CostEstimate(flops=12 * 10**9, bytes_accessed=15 * 10**6, transcendentals=300000),
        name="expert_layer",
    )(expert_ids.T, route_gates.T, activations, cotangent, gate_proj, up_proj, down_proj, *constants())
    kept = jax.ShapeDtypeStruct((1, DC, FF), BF16)
    return pl.pallas_call(
        place,
        out_shape=(tokens,) * 2 + (kept,) * 3,
        in_specs=[vmem] * 5,
        out_specs=(anywhere,) * 5,
        scratch_shapes=[dma((5,))],
        compiler_params=pltpu.CompilerParams(vmem_limit_bytes=2**20),
        name="place",
    )(*out)


def solution(mesh):
    in_specs = (
        P(("dp", "expert"), None),
        P(("dp", "expert"), None),
        P(("dp", "expert"), None),
        P("expert", None, None),
        P("expert", None, None),
        P("expert", None, None),
        P(("dp", "expert"), None),
    )
    out_specs = (
        P(("dp", "expert"), None),
        P(("dp", "expert"), None),
        P("expert", "dp", None),
        P("expert", "dp", None),
        P("expert", "dp", None),
    )
    return jax.shard_map(shards, mesh=mesh, in_specs=in_specs, out_specs=out_specs, check_vma=False)
```

```python
import functools

import jax
import jax.numpy as jnp
import numpy as np
from jax import lax
from jax.experimental import pallas as pl
from jax.experimental.pallas import tpu as pltpu
from jax.sharding import PartitionSpec as P

MESH = pl.DeviceIdType.MESH
BF16 = jnp.bfloat16
F32 = jnp.float32

CAP = 12
NE = 32
ND = 8
TOK = 128
TOP = 8
D = 2048
FF = 768
SLOTS = NE * CAP
GROUP = 8
NG = NE // GROUP
NQ = 4
QW = D // NQ
GR = GROUP * CAP
PIECE = 16
NP = CAP * NQ // PIECE
ORDER = sorted(range(1, NE), key=lambda o: (o % 2, -abs(2 - abs(2 - o // 8)) - abs(2 - abs(2 - o // 2 % 4)), 2 - abs(2 - o // 8), o))
STAGES = ((0, 1), (1, 3), (3, 6))
OFFSETS = (4, 3, -3, 2, -2, 1, -1, 0)
LINKS = ND - 1
DC = D // ND
HALF = FF // 2
TILE = 256


def dot(a, b):
    return jnp.dot(a, b, preferred_element_type=F32)


def dot_t(a, b):
    return lax.dot_general(a, b, (((1,), (1,)), ((), ())), preferred_element_type=F32)


def constants():
    table = np.zeros((NP, GROUP * PIECE, 2 * GR), np.float32)
    for p in range(NP):
        for s in range(GROUP):
            for u in range(PIECE):
                q, r = divmod(p * PIECE + u, CAP)
                table[p, s * PIECE + u, (q - p) * GR + s * CAP + r] = 1.0
    return jnp.asarray(table, BF16), jnp.asarray(table.transpose(0, 2, 1), BF16)


def kernel(
    ids_hbm, gates_hbm, act_hbm, cot_hbm, wg_hbm, wu_hbm, wd_hbm, to_hbm, from_hbm,
    lo_ref, gi_ref, gg_ref, gu_ref, gd_ref,
    ids_ref, gates_ref, act, cot, wg, wu, wd, to_piece, from_piece, pick, sgate, comb, send, recv, c_send, c_recv, stack, x_rows, c_rows,
    lt, fac, hid, rs_send, rs_recv, met,
    wsem, lsem, ssem, rsem, csem, crem, zs, zr,
):
    me = lax.axis_index("expert")
    z = lax.axis_index("dp")
    my_y, my_x, my_c = me // 8, (me // 2) % 4, me % 2

    def peer(o):
        return (((my_y + o // 8) % 4) * 4 + (my_x + (o // 2) % 4) % 4) * 2 + (my_c + o % 2) % 2

    sources = (
        (ids_hbm, ids_ref), (gates_hbm, gates_ref), (act_hbm, act), (to_hbm, to_piece), (cot_hbm, cot),
        (from_hbm, from_piece), (wg_hbm.at[0], wg), (wu_hbm.at[0], wu), (wd_hbm.at[0], wd),
    )
    loads = [pltpu.make_async_copy(a, b, wsem.at[i]) for i, (a, b) in enumerate(sources)]
    for load in loads[:4]:
        load.start()

    barrier = pltpu.get_barrier_semaphore()

    def greet(o, _):
        pl.semaphore_signal(barrier, inc=1, device_id={"expert": peer(o)}, device_id_type=MESH)
        return 0

    lax.fori_loop(1, NE, greet, 0)
    for step in (1, ND - 1):
        pl.semaphore_signal(barrier, inc=1, device_id={"dp": (z + step) % ND}, device_id_type=MESH)
    for load in loads[4:]:
        load.start()

    def over_peers(f):
        for n, o in enumerate(ORDER):
            f(n, o)

    def mirror(o):
        return ((4 - o // 8) % 4 * 4 + (4 - o // 2 % 4) % 4) * 2 + o % 2

    def exchange(p, to, source, held, sem):
        return pltpu.make_async_remote_copy(
            src_ref=send.at[p, source],
            dst_ref=recv.at[p, held],
            send_sem=ssem.at[p],
            recv_sem=rsem.at[sem],
            device_id={"expert": to},
            device_id_type=MESH,
        )

    def dispatch(n, o):
        to = peer(o)
        return exchange(0, to, to, n, n // GROUP)

    def arrived(g):
        count = GROUP if g < NG - 1 else GROUP - 1
        return exchange(0, peer(1), pl.ds(0, count), pl.ds(g * GROUP, count), g)

    def send_back(p, n, o):
        return exchange(p, peer(mirror(o)), n, me, NG - 1 + p)

    def all_of(p):
        some = pl.ds(0, NE - 1)
        return exchange(p, peer(1), some, some, NG - 1 + p)

    def cot_blocks(t, to, source, held):
        start, end = STAGES[t]
        pieces = pl.ds(start, end - start)
        return pltpu.make_async_remote_copy(
            src_ref=c_send.at[source, pieces],
            dst_ref=c_recv.at[held, pieces],
            send_sem=csem.at[t],
            recv_sem=crem.at[t],
            device_id={"expert": to},
            device_id_type=MESH,
        )

    def dispatch_cot(t, n, o):
        to = peer(o)
        return cot_blocks(t, to, to, n)

    def all_of_cot(t):
        some = pl.ds(0, NE - 1)
        return cot_blocks(t, peer(1), some, some)

    def own(p):
        source, held = (me, NE - 1) if p == 0 else (NE - 1, me)
        return pltpu.make_async_copy(send.at[p, source], recv.at[p, held], lsem.at[p])

    own_cot = pltpu.make_async_copy(c_send.at[me], c_recv.at[NE - 1], lsem.at[3])

    def links(source, held, sem, d):
        return pltpu.make_async_remote_copy(
            src_ref=source,
            dst_ref=held,
            send_sem=zs,
            recv_sem=sem,
            device_id={"dp": (z + 1 - 2 * d + ND) % ND},
            device_id_type=MESH,
        )

    def link(m, d, i):
        return links(rs_send.at[m, d, i], rs_recv.at[m, d, i], zr.at[m, d, i], d)

    chunks = [(z + off + ND) % ND for off in OFFSETS]

    loads[0].wait()
    loads[1].wait()
    ids = ids_ref[...]
    gates = gates_ref[...]
    experts = lax.broadcasted_iota(jnp.int32, (NE, TOK), 0)
    named = jnp.zeros((NE, TOK), F32)
    gate_of = jnp.zeros((NE, TOK), F32)
    for k in range(TOP):
        hit = ids[k : k + 1, :] == experts
        named = named + jnp.where(hit, 1.0, 0.0)
        gate_of = gate_of + jnp.where(hit, gates[k : k + 1, :], 0.0)
    before = lax.broadcasted_iota(jnp.int32, (TOK, TOK), 0) < lax.broadcasted_iota(jnp.int32, (TOK, TOK), 1)
    earlier = dot(named.astype(BF16), jnp.where(before, 1.0, 0.0).astype(BF16))
    slot_of = jnp.where(named > 0.0, earlier, -1.0).astype(BF16)
    slots = lax.broadcasted_iota(jnp.int32, (SLOTS, NE), 0)
    first_slot = lax.broadcasted_iota(jnp.int32, (SLOTS, NE), 1) * CAP
    expand = jnp.where((slots >= first_slot) & (slots < first_slot + CAP), 1.0, 0.0)
    row = jnp.sum(expand * (slots - first_slot).astype(F32), axis=1, keepdims=True)
    expand = expand.astype(BF16)
    match = dot(expand, slot_of) == row
    high = gate_of.astype(BF16)
    rest = gate_of - high.astype(F32)
    mid = rest.astype(BF16)
    low = (rest - mid.astype(F32)).astype(BF16)
    ones = jnp.where(match, 1.0, 0.0)
    pick[...] = ones.astype(BF16)

    def shuffle_out(p, g, block):
        for t in range(NP):
            both = jnp.concatenate([block(t), block(t + 1)], axis=0)
            packed = dot(to_piece[t], both).astype(BF16)
            send[p, g * GROUP : (g + 1) * GROUP, t] = packed.reshape(GROUP, PIECE, QW)

    def unshuffle(p, g):
        def piece(t):
            return recv[p, g * GROUP : (g + 1) * GROUP, t].reshape(GROUP * PIECE, QW)

        for q in range(NQ):
            total = None
            if q < NP:
                total = dot(from_piece[q, :GR, :], piece(q))
            if q > 0:
                more = dot(from_piece[q - 1, GR:, :], piece(q - 1))
                total = more if total is None else total + more
            x_rows[g * GR : (g + 1) * GR, q * QW : (q + 1) * QW] = total.astype(BF16)

    loads[2].wait()
    loads[3].wait()
    for g in range(NG):
        rows = dot(pick[g * GR : (g + 1) * GR, :], act[...]).astype(BF16)
        shuffle_out(0, g, lambda q: rows[:, q * QW : (q + 1) * QW])
    pl.semaphore_wait(barrier, NE - 1 + 2)
    over_peers(lambda n, o: dispatch(n, o).start())
    own(0).start()

    spread = dot(expand, high) + dot(expand, mid) + dot(expand, low)
    weight = jnp.where(match, spread, 0.0)
    sgate[...] = jnp.sum(weight, axis=1, keepdims=True)
    weight_t = weight.T
    weight_high = weight_t.astype(BF16)
    comb[0] = weight_high
    comb[1] = (weight_t - weight_high.astype(F32)).astype(BF16)
    comb[2] = ones.T.astype(BF16)

    loads[4].wait()
    for g in range(NG):
        picked, gate = pick[g * GR : (g + 1) * GR, :], sgate[g * GR : (g + 1) * GR, :]
        blocks = [
            (dot(picked, cot[:, pl.ds(pl.multiple_of(c * DC, DC), DC)]) * gate).astype(BF16) for c in chunks
        ]
        for p in range(2 * NP):
            q = p + p // NP
            both = jnp.concatenate([blocks[q], blocks[q + 1]], axis=0)
            packed = dot(to_piece[p % NP], both).astype(BF16)
            c_send[g * GROUP : (g + 1) * GROUP, p] = packed.reshape(GROUP, PIECE, DC)
    own_cot.start()

    for t in (0, 1):
        over_peers(lambda n, o: dispatch_cot(t, n, o).start())

    for load in loads[5:]:
        load.wait()
    def put_hidden(m, n, value, rows=slice(0, SLOTS)):
        for at in range(n * TILE, (n + 1) * TILE, 128):
            d, col = at // HALF, at % HALF
            hid[m, d, rows, col : col + 128] = value[:, at - n * TILE : at - n * TILE + 128]

    for half in range(2):
        for g in ((0, 1, 2), (3,))[half]:
            arrived(g).wait_recv()
            if g == NG - 1:
                own(0).wait()
            unshuffle(0, g)
        if half == 1:
            over_peers(lambda n, o: dispatch_cot(2, n, o).start())
        rows = slice(half * 3 * GR, (3 + half) * GR)
        for n in range(FF // TILE):
            cols = slice(n * TILE, (n + 1) * TILE)
            gate_pre = dot(x_rows[rows, :], wg[:, cols])
            up_pre = dot(x_rows[rows, :], wu[:, cols])
            sig = 1.0 / (1.0 + jnp.exp(-gate_pre))
            silu = gate_pre * sig
            fac[0, rows, cols] = silu
            fac[1, rows, cols] = up_pre * sig * (1.0 + gate_pre * (1.0 - sig))
            put_hidden(0, n, (silu * up_pre).astype(BF16), rows)

    def take_cot(q):
        at = pl.ds(pl.multiple_of(chunks[q] * DC, DC), DC)
        base, i = NP * (q // NQ), q % NQ
        for g in range(NG):
            def piece(p):
                return c_recv[g * GROUP : (g + 1) * GROUP, p].reshape(GROUP * PIECE, DC)

            total = None
            if i < NP:
                total = dot(from_piece[i, :GR, :], piece(base + i))
            if i > 0:
                more = dot(from_piece[i - 1, GR:, :], piece(base + i - 1))
                total = more if total is None else total + more
            c_rows[g * GR : (g + 1) * GR, at] = total.astype(BF16)
        lt[0, chunks[q]] = c_rows[:, at].T

    def part(m, h, c):
        return dot(lt[(m + 1) // 2, c], hid[m, h])

    def chunk(d, i):
        return (z + (1 - 2 * d) * (4 - (i + 1) // 2) + ND) % ND

    def first(m, d, i):
        rs_send[m, d, i] = part(m, (d + i) % 2, chunk(d, i)).astype(BF16)
        link(m, d, i).start()

    def then(m, d, i):
        mine = part(m, (d + i) % 2, chunk(d, i))
        link(m, d, i - 2).wait_recv()
        rs_send[m, d, i] = (mine + rs_recv[m, d, i - 2].astype(F32)).astype(BF16)
        link(m, d, i).start()

    def begin(lowest, count, i):
        def body(j, _):
            first(lowest + j // 2, j % 2, i)
            return 0

        lax.fori_loop(0, 2 * count, body, 0)

    def both_ways(m, i):
        def body(d, _):
            then(m, d, i)
            return 0

        lax.fori_loop(0, 2, body, 0)

    def rounds(start, end):
        def body(j, _):
            m = (j // 2) % 3
            then(m, j % 2, 2 + j // 6 + 2 * ((2 - m) // 2))
            return 0

        lax.fori_loop(6 * start, 6 * end, body, 0)

    def late_rounds(start, end):
        def body(j, _):
            then(1 + (j // 2) % 2, j % 2, 2 + j // 4)
            return 0

        lax.fori_loop(4 * start, 4 * end, body, 0)

    all_of_cot(0).wait_recv()
    own_cot.wait()
    take_cot(0)
    begin(0, 1, 0)

    def whole(m):
        return jnp.concatenate([hid[m, 0], hid[m, 1]], axis=1)

    def stack_rows(q, rows):
        for g in range(NG):
            stack[g, q] = rows[g * GR : (g + 1) * GR].astype(BF16)

    for q in range(NQ):
        stack_rows(q, dot_t(whole(0), wd[q * QW : (q + 1) * QW, :]))
    for g in range(NG):
        shuffle_out(1, g, lambda q: stack[g, q])

    for j in range(ND):
        lt[1, j] = x_rows[:, j * DC : (j + 1) * DC].T
    all_of_cot(1).wait_recv()
    for q in (1, 2):
        take_cot(q)
    begin(0, 1, 1)
    take_cot(3)
    both_ways(0, 2)
    all_of_cot(2).wait_recv()
    for q in (4, 5, 6, 7):
        take_cot(q)
    over_peers(lambda n, o: send_back(1, n, o).start())
    own(1).start()
    both_ways(0, 3)

    for n in range(FF // TILE):
        cols = slice(n * TILE, (n + 1) * TILE)
        back = dot(c_rows[...], wd[:, cols])
        put_hidden(2, n, (back * fac[0, :, cols]).astype(BF16))
        put_hidden(1, n, (back * fac[1, :, cols]).astype(BF16))
    begin(1, 2, 0)
    begin(1, 2, 1)

    for q in range(NQ):
        rows = slice(q * QW, (q + 1) * QW)
        stack_rows(q, dot_t(whole(1), wg[rows, :]) + dot_t(whole(2), wu[rows, :]))
    for g in range(NG):
        shuffle_out(2, g, lambda q: stack[g, q])
    over_peers(lambda n, o: send_back(2, n, o).start())
    own(2).start()

    rounds(0, 2)
    all_of(1).wait_recv()
    own(1).wait()
    for g in range(NG):
        unshuffle(1, g)
    for q in range(NQ):
        cols = slice(q * QW, (q + 1) * QW)
        lo_ref[:, cols] = (dot(comb[0], x_rows[:, cols]) + dot(comb[1], x_rows[:, cols])).astype(BF16)

    rounds(2, 3)
    all_of(2).wait_recv()
    own(2).wait()
    for g in range(NG):
        unshuffle(2, g)
    for q in range(NQ):
        cols = slice(q * QW, (q + 1) * QW)
        gi_ref[:, cols] = dot(comb[2], x_rows[:, cols]).astype(BF16)

    def meet(m):
        for h in range(2):
            mine = part(m, h, z)
            link(m, 1 - h, LINKS - 2).wait_recv()
            met[m, h] = mine + rs_recv[m, 1 - h, LINKS - 2].astype(F32)

    def finish(m, out):
        for h in range(2):
            link(m, h, LINKS - 1).wait_recv()
            total = met[m, h] + rs_recv[m, h, LINKS - 1].astype(F32)
            out[:, h * HALF : (h + 1) * HALF] = total.astype(BF16)

    late_rounds(3, 4)
    meet(0)
    finish(0, gd_ref)
    late_rounds(4, 5)
    meet(1)
    meet(2)
    for p in range(3):
        all_of(p).wait_send()
    for t in range(len(STAGES)):
        all_of_cot(t).wait_send()
    finish(1, gg_ref)
    finish(2, gu_ref)

    links(rs_send, rs_recv, zr.at[0, 0, 0], 0).wait_send()


def place(*refs):
    ins, outs, sem = refs[:5], refs[5:10], refs[10]
    stores = []
    for i in range(5):
        rows = ins[i].shape[0] // 2
        for h in range(2):
            some = pl.ds(h * rows, rows)
            out = outs[i].at[some] if i < 2 else outs[i].at[0, some]
            stores.append(pltpu.make_async_copy(ins[i].at[some], out, sem.at[2 * i + h]))
    for store in stores:
        store.start()
    for store in stores:
        store.wait()


def shards(activations, expert_ids, route_gates, gate_proj, up_proj, down_proj, cotangent):
    vmem = pl.BlockSpec(memory_space=pltpu.VMEM)
    anywhere = pl.BlockSpec(memory_space=pl.ANY)
    dma = pltpu.SemaphoreType.DMA
    tokens = jax.ShapeDtypeStruct((TOK, D), BF16)
    grads = jax.ShapeDtypeStruct((DC, FF), BF16)
    out = pl.pallas_call(
        kernel,
        out_shape=tuple(pltpu.VMEM(s.shape, BF16) for s in (tokens,) * 2 + (grads,) * 3),
        in_specs=[anywhere] * 9,
        out_specs=(vmem,) * 5,
        scratch_shapes=[
            pltpu.VMEM((TOP, TOK), jnp.int32),
            pltpu.VMEM((TOP, TOK), F32),
            pltpu.VMEM((TOK, D), BF16),
            pltpu.VMEM((TOK, D), BF16),
            pltpu.VMEM((D, FF), BF16),
            pltpu.VMEM((D, FF), BF16),
            pltpu.VMEM((D, FF), BF16),
            pltpu.VMEM((NP, GROUP * PIECE, 2 * GR), BF16),
            pltpu.VMEM((NP, 2 * GR, GROUP * PIECE), BF16),
            pltpu.VMEM((SLOTS, TOK), BF16),
            pltpu.VMEM((SLOTS, 1), F32),
            pltpu.VMEM((3, TOK, SLOTS), BF16),
            pltpu.VMEM((3, NE, NP, PIECE, QW), BF16),
            pltpu.VMEM((3, NE, NP, PIECE, QW), BF16),
            pltpu.VMEM((NE, 2 * NP, PIECE, DC), BF16),
            pltpu.VMEM((NE, 2 * NP, PIECE, DC), BF16),
            pltpu.VMEM((NG, NQ, GR, QW), BF16),
            pltpu.VMEM((SLOTS, D), BF16),
            pltpu.VMEM((SLOTS, D), BF16),
            pltpu.VMEM((2, ND, DC, SLOTS), BF16),
            pltpu.VMEM((2, SLOTS, FF), F32),
            pltpu.VMEM((3, 2, SLOTS, HALF), BF16),
            pltpu.VMEM((3, 2, LINKS, DC, HALF), BF16),
            pltpu.VMEM((3, 2, LINKS, DC, HALF), BF16),
            pltpu.VMEM((3, 2, DC, HALF), F32),
            dma((9,)),
            dma((4,)),
            dma((3,)),
            dma((NG + 2,)),
            dma((len(STAGES),)),
            dma((len(STAGES),)),
            dma,
            dma((3, 2, LINKS)),
        ],
        compiler_params=pltpu.CompilerParams(
            collective_id=0, has_side_effects=True, vmem_limit_bytes=54 * 2**20
        ),
        cost_estimate=pl.CostEstimate(flops=12 * 10**9, bytes_accessed=15 * 10**6, transcendentals=300000),
        name="expert_layer",
    )(expert_ids.T, route_gates.T, activations, cotangent, gate_proj, up_proj, down_proj, *constants())
    kept = jax.ShapeDtypeStruct((1, DC, FF), BF16)
    return pl.pallas_call(
        place,
        out_shape=(tokens,) * 2 + (kept,) * 3,
        in_specs=[vmem] * 5,
        out_specs=(anywhere,) * 5,
        scratch_shapes=[dma((10,))],
        compiler_params=pltpu.CompilerParams(vmem_limit_bytes=2**20),
        name="place",
    )(*out)


def solution(mesh):
    in_specs = (
        P(("dp", "expert"), None),
        P(("dp", "expert"), None),
        P(("dp", "expert"), None),
        P("expert", None, None),
        P("expert", None, None),
        P("expert", None, None),
        P(("dp", "expert"), None),
    )
    out_specs = (
        P(("dp", "expert"), None),
        P(("dp", "expert"), None),
        P("expert", "dp", None),
        P("expert", "dp", None),
        P("expert", "dp", None),
    )
    return jax.shard_map(shards, mesh=mesh, in_specs=in_specs, out_specs=out_specs, check_vma=False)
```

```python
import functools

import jax
import jax.numpy as jnp
import numpy as np
from jax import lax
from jax.experimental import pallas as pl
from jax.experimental.pallas import tpu as pltpu
from jax.sharding import PartitionSpec as P

MESH = pl.DeviceIdType.MESH
BF16 = jnp.bfloat16
F32 = jnp.float32

CAP = 12
NE = 32
ND = 8
TOK = 128
TOP = 8
D = 2048
FF = 768
SLOTS = NE * CAP
GROUP = 8
NG = NE // GROUP
NQ = 4
QW = D // NQ
GR = GROUP * CAP
PIECE = 16
NP = CAP * NQ // PIECE
ORDER = sorted(range(1, NE), key=lambda o: (o % 2, -abs(2 - abs(2 - o // 8)) - abs(2 - abs(2 - o // 2 % 4)), 2 - abs(2 - o // 8), o))
STAGES = ((0, 1), (1, 3), (3, 6))
OFFSETS = (4, 3, -3, 2, -2, 1, -1, 0)
LINKS = ND - 1
DC = D // ND
HALF = FF // 2
TILE = 256


def dot(a, b):
    return jnp.dot(a, b, preferred_element_type=F32)


def dot_t(a, b):
    return lax.dot_general(a, b, (((1,), (1,)), ((), ())), preferred_element_type=F32)


def constants():
    table = np.zeros((NP, GROUP * PIECE, 2 * GR), np.float32)
    for p in range(NP):
        for s in range(GROUP):
            for u in range(PIECE):
                q, r = divmod(p * PIECE + u, CAP)
                table[p, s * PIECE + u, (q - p) * GR + s * CAP + r] = 1.0
    return jnp.asarray(table, BF16), jnp.asarray(table.transpose(0, 2, 1), BF16)


def kernel(
    ids_hbm, gates_hbm, act_hbm, cot_hbm, wg_hbm, wu_hbm, wd_hbm, to_hbm, from_hbm,
    lo_ref, gi_ref, gg_ref, gu_ref, gd_ref,
    ids_ref, gates_ref, act, cot, wg, wu, wd, to_piece, from_piece, pick, sgate, comb, send, recv, c_send, c_recv, stack, x_rows, c_rows,
    lt, fac, hid, rs_send, rs_recv, met,
    wsem, lsem, ssem, rsem, csem, crem, zs, zr,
):
    me = lax.axis_index("expert")
    z = lax.axis_index("dp")
    my_y, my_x, my_c = me // 8, (me // 2) % 4, me % 2

    def peer(o):
        return (((my_y + o // 8) % 4) * 4 + (my_x + (o // 2) % 4) % 4) * 2 + (my_c + o % 2) % 2

    sources = (
        (ids_hbm, ids_ref), (gates_hbm, gates_ref), (act_hbm, act), (to_hbm, to_piece), (cot_hbm, cot),
        (from_hbm, from_piece), (wg_hbm.at[0], wg), (wu_hbm.at[0], wu), (wd_hbm.at[0], wd),
    )
    loads = [pltpu.make_async_copy(a, b, wsem.at[i]) for i, (a, b) in enumerate(sources)]
    for load in loads[:4]:
        load.start()

    barrier = pltpu.get_barrier_semaphore()

    def greet(o, _):
        pl.semaphore_signal(barrier, inc=1, device_id={"expert": peer(o)}, device_id_type=MESH)
        return 0

    lax.fori_loop(1, NE, greet, 0)
    for step in (1, ND - 1):
        pl.semaphore_signal(barrier, inc=1, device_id={"dp": (z + step) % ND}, device_id_type=MESH)
    for load in loads[4:]:
        load.start()

    def over_peers(f):
        for n, o in enumerate(ORDER):
            f(n, o)

    def mirror(o):
        return ((4 - o // 8) % 4 * 4 + (4 - o // 2 % 4) % 4) * 2 + o % 2

    def exchange(p, to, source, held, sem):
        return pltpu.make_async_remote_copy(
            src_ref=send.at[p, source],
            dst_ref=recv.at[p, held],
            send_sem=ssem.at[p],
            recv_sem=rsem.at[sem],
            device_id={"expert": to},
            device_id_type=MESH,
        )

    def dispatch(n, o):
        to = peer(o)
        return exchange(0, to, to, n, n // GROUP)

    def arrived(g):
        count = GROUP if g < NG - 1 else GROUP - 1
        return exchange(0, peer(1), pl.ds(0, count), pl.ds(g * GROUP, count), g)

    def send_back(p, n, o):
        return exchange(p, peer(mirror(o)), n, me, NG - 1 + p)

    def all_of(p):
        some = pl.ds(0, NE - 1)
        return exchange(p, peer(1), some, some, NG - 1 + p)

    def cot_blocks(t, to, source, held):
        start, end = STAGES[t]
        pieces = pl.ds(start, end - start)
        return pltpu.make_async_remote_copy(
            src_ref=c_send.at[source, pieces],
            dst_ref=c_recv.at[held, pieces],
            send_sem=csem.at[t],
            recv_sem=crem.at[t],
            device_id={"expert": to},
            device_id_type=MESH,
        )

    def dispatch_cot(t, n, o):
        to = peer(o)
        return cot_blocks(t, to, to, n)

    def all_of_cot(t):
        some = pl.ds(0, NE - 1)
        return cot_blocks(t, peer(1), some, some)

    def own(p):
        source, held = (me, NE - 1) if p == 0 else (NE - 1, me)
        return pltpu.make_async_copy(send.at[p, source], recv.at[p, held], lsem.at[p])

    own_cot = pltpu.make_async_copy(c_send.at[me], c_recv.at[NE - 1], lsem.at[3])

    def links(source, held, sem, d):
        return pltpu.make_async_remote_copy(
            src_ref=source,
            dst_ref=held,
            send_sem=zs,
            recv_sem=sem,
            device_id={"dp": (z + 1 - 2 * d + ND) % ND},
            device_id_type=MESH,
        )

    def link(kind, d, i):
        some = pl.ds(kind, 1 + kind)
        return links(rs_send.at[d, i, some], rs_recv.at[d, i, some], zr.at[kind, d, i], d)

    def members(kind):
        return (1, 2) if kind else (0,)

    chunks = [(z + off + ND) % ND for off in OFFSETS]

    loads[0].wait()
    loads[1].wait()
    ids = ids_ref[...]
    gates = gates_ref[...]
    experts = lax.broadcasted_iota(jnp.int32, (NE, TOK), 0)
    named = jnp.zeros((NE, TOK), F32)
    gate_of = jnp.zeros((NE, TOK), F32)
    for k in range(TOP):
        hit = ids[k : k + 1, :] == experts
        named = named + jnp.where(hit, 1.0, 0.0)
        gate_of = gate_of + jnp.where(hit, gates[k : k + 1, :], 0.0)
    before = lax.broadcasted_iota(jnp.int32, (TOK, TOK), 0) < lax.broadcasted_iota(jnp.int32, (TOK, TOK), 1)
    earlier = dot(named.astype(BF16), jnp.where(before, 1.0, 0.0).astype(BF16))
    slot_of = jnp.where(named > 0.0, earlier, -1.0).astype(BF16)
    slots = lax.broadcasted_iota(jnp.int32, (SLOTS, NE), 0)
    first_slot = lax.broadcasted_iota(jnp.int32, (SLOTS, NE), 1) * CAP
    expand = jnp.where((slots >= first_slot) & (slots < first_slot + CAP), 1.0, 0.0)
    row = jnp.sum(expand * (slots - first_slot).astype(F32), axis=1, keepdims=True)
    expand = expand.astype(BF16)
    match = dot(expand, slot_of) == row
    high = gate_of.astype(BF16)
    rest = gate_of - high.astype(F32)
    mid = rest.astype(BF16)
    low = (rest - mid.astype(F32)).astype(BF16)
    ones = jnp.where(match, 1.0, 0.0)
    pick[...] = ones.astype(BF16)

    def shuffle_out(p, g, block):
        for t in range(NP):
            both = jnp.concatenate([block(t), block(t + 1)], axis=0)
            packed = dot(to_piece[t], both).astype(BF16)
            send[p, g * GROUP : (g + 1) * GROUP, t] = packed.reshape(GROUP, PIECE, QW)

    def unshuffle(p, g):
        def piece(t):
            return recv[p, g * GROUP : (g + 1) * GROUP, t].reshape(GROUP * PIECE, QW)

        for q in range(NQ):
            total = None
            if q < NP:
                total = dot(from_piece[q, :GR, :], piece(q))
            if q > 0:
                more = dot(from_piece[q - 1, GR:, :], piece(q - 1))
                total = more if total is None else total + more
            x_rows[g * GR : (g + 1) * GR, q * QW : (q + 1) * QW] = total.astype(BF16)

    loads[2].wait()
    loads[3].wait()
    for g in range(NG):
        rows = dot(pick[g * GR : (g + 1) * GR, :], act[...]).astype(BF16)
        shuffle_out(0, g, lambda q: rows[:, q * QW : (q + 1) * QW])
    pl.semaphore_wait(barrier, NE - 1 + 2)
    over_peers(lambda n, o: dispatch(n, o).start())
    own(0).start()

    spread = dot(expand, high) + dot(expand, mid) + dot(expand, low)
    weight = jnp.where(match, spread, 0.0)
    sgate[...] = jnp.sum(weight, axis=1, keepdims=True)
    weight_t = weight.T
    weight_high = weight_t.astype(BF16)
    comb[0] = weight_high
    comb[1] = (weight_t - weight_high.astype(F32)).astype(BF16)
    comb[2] = ones.T.astype(BF16)

    loads[4].wait()
    for g in range(NG):
        picked, gate = pick[g * GR : (g + 1) * GR, :], sgate[g * GR : (g + 1) * GR, :]
        blocks = [
            (dot(picked, cot[:, pl.ds(pl.multiple_of(c * DC, DC), DC)]) * gate).astype(BF16) for c in chunks
        ]
        for p in range(2 * NP):
            q = p + p // NP
            both = jnp.concatenate([blocks[q], blocks[q + 1]], axis=0)
            packed = dot(to_piece[p % NP], both).astype(BF16)
            c_send[g * GROUP : (g + 1) * GROUP, p] = packed.reshape(GROUP, PIECE, DC)
    own_cot.start()

    for t in (0, 1):
        over_peers(lambda n, o: dispatch_cot(t, n, o).start())

    for load in loads[5:]:
        load.wait()
    def put_hidden(m, n, value, rows=slice(0, SLOTS)):
        for at in range(n * TILE, (n + 1) * TILE, 128):
            d, col = at // HALF, at % HALF
            hid[m, d, rows, col : col + 128] = value[:, at - n * TILE : at - n * TILE + 128]

    for half in range(2):
        for g in ((0, 1, 2), (3,))[half]:
            arrived(g).wait_recv()
            if g == NG - 1:
                own(0).wait()
            unshuffle(0, g)
        if half == 1:
            over_peers(lambda n, o: dispatch_cot(2, n, o).start())
        rows = slice(half * 3 * GR, (3 + half) * GR)
        for n in range(FF // TILE):
            cols = slice(n * TILE, (n + 1) * TILE)
            gate_pre = dot(x_rows[rows, :], wg[:, cols])
            up_pre = dot(x_rows[rows, :], wu[:, cols])
            sig = 1.0 / (1.0 + jnp.exp(-gate_pre))
            silu = gate_pre * sig
            fac[0, rows, cols] = silu
            fac[1, rows, cols] = up_pre * sig * (1.0 + gate_pre * (1.0 - sig))
            put_hidden(0, n, (silu * up_pre).astype(BF16), rows)

    def take_cot(q):
        at = pl.ds(pl.multiple_of(chunks[q] * DC, DC), DC)
        base, i = NP * (q // NQ), q % NQ
        for g in range(NG):
            def piece(p):
                return c_recv[g * GROUP : (g + 1) * GROUP, p].reshape(GROUP * PIECE, DC)

            total = None
            if i < NP:
                total = dot(from_piece[i, :GR, :], piece(base + i))
            if i > 0:
                more = dot(from_piece[i - 1, GR:, :], piece(base + i - 1))
                total = more if total is None else total + more
            c_rows[g * GR : (g + 1) * GR, at] = total.astype(BF16)
        lt[0, chunks[q]] = c_rows[:, at].T

    def part(m, h, c):
        return dot(lt[(m + 1) // 2, c], hid[m, h])

    def chunk(d, i):
        return (z + (1 - 2 * d) * (4 - (i + 1) // 2) + ND) % ND

    def first(kind, d, i):
        for m in members(kind):
            rs_send[d, i, m] = part(m, (d + i) % 2, chunk(d, i)).astype(BF16)
        link(kind, d, i).start()

    def then(kind, d, i):
        link(kind, d, i - 2).wait_recv()
        for m in members(kind):
            mine = part(m, (d + i) % 2, chunk(d, i))
            rs_send[d, i, m] = (mine + rs_recv[d, i - 2, m].astype(F32)).astype(BF16)
        link(kind, d, i).start()

    def begin(kind, i):
        def body(d, _):
            first(kind, d, i)
            return 0

        lax.fori_loop(0, 2, body, 0)

    def both_ways(kind, i):
        def body(d, _):
            then(kind, d, i)
            return 0

        lax.fori_loop(0, 2, body, 0)

    def rounds(start, end):
        def body(j, _):
            then(0, j % 2, 4 + j // 2)
            then(1, j % 2, 2 + j // 2)
            return 0

        lax.fori_loop(2 * start, 2 * end, body, 0)

    def late_rounds(start, end):
        def body(j, _):
            then(1, j % 2, 2 + j // 2)
            return 0

        lax.fori_loop(2 * start, 2 * end, body, 0)

    all_of_cot(0).wait_recv()
    own_cot.wait()
    take_cot(0)
    begin(0, 0)

    def whole(m):
        return jnp.concatenate([hid[m, 0], hid[m, 1]], axis=1)

    def stack_rows(q, rows):
        for g in range(NG):
            stack[g, q] = rows[g * GR : (g + 1) * GR].astype(BF16)

    for q in range(NQ):
        stack_rows(q, dot_t(whole(0), wd[q * QW : (q + 1) * QW, :]))
    for g in range(NG):
        shuffle_out(1, g, lambda q: stack[g, q])

    for j in range(ND):
        lt[1, j] = x_rows[:, j * DC : (j + 1) * DC].T
    all_of_cot(1).wait_recv()
    for q in (1, 2):
        take_cot(q)
    begin(0, 1)
    take_cot(3)
    both_ways(0, 2)
    all_of_cot(2).wait_recv()
    for q in (4, 5, 6, 7):
        take_cot(q)
    over_peers(lambda n, o: send_back(1, n, o).start())
    own(1).start()
    both_ways(0, 3)

    for n in range(FF // TILE):
        cols = slice(n * TILE, (n + 1) * TILE)
        back = dot(c_rows[...], wd[:, cols])
        put_hidden(2, n, (back * fac[0, :, cols]).astype(BF16))
        put_hidden(1, n, (back * fac[1, :, cols]).astype(BF16))
    begin(1, 0)
    begin(1, 1)

    for q in range(NQ):
        rows = slice(q * QW, (q + 1) * QW)
        stack_rows(q, dot_t(whole(1), wg[rows, :]) + dot_t(whole(2), wu[rows, :]))
    for g in range(NG):
        shuffle_out(2, g, lambda q: stack[g, q])
    over_peers(lambda n, o: send_back(2, n, o).start())
    own(2).start()

    rounds(0, 2)
    all_of(1).wait_recv()
    own(1).wait()
    for g in range(NG):
        unshuffle(1, g)
    for q in range(NQ):
        cols = slice(q * QW, (q + 1) * QW)
        lo_ref[:, cols] = (dot(comb[0], x_rows[:, cols]) + dot(comb[1], x_rows[:, cols])).astype(BF16)

    rounds(2, 3)
    all_of(2).wait_recv()
    own(2).wait()
    for g in range(NG):
        unshuffle(2, g)
    for q in range(NQ):
        cols = slice(q * QW, (q + 1) * QW)
        gi_ref[:, cols] = dot(comb[2], x_rows[:, cols]).astype(BF16)

    def meet(kind):
        for h in range(2):
            link(kind, 1 - h, LINKS - 2).wait_recv()
            for m in members(kind):
                met[m % 2, h] = part(m, h, z) + rs_recv[1 - h, LINKS - 2, m].astype(F32)

    def finish(kind):
        for h in range(2):
            link(kind, h, LINKS - 1).wait_recv()
            for m in members(kind):
                total = met[m % 2, h] + rs_recv[h, LINKS - 1, m].astype(F32)
                (gd_ref, gg_ref, gu_ref)[m][:, h * HALF : (h + 1) * HALF] = total.astype(BF16)

    late_rounds(3, 4)
    meet(0)
    finish(0)
    late_rounds(4, 5)
    meet(1)
    for p in range(3):
        all_of(p).wait_send()
    for t in range(len(STAGES)):
        all_of_cot(t).wait_send()
    finish(1)

    links(rs_send, rs_recv, zr.at[0, 0, 0], 0).wait_send()


def place(*refs):
    ins, outs, sem = refs[:5], refs[5:10], refs[10]
    stores = []
    for i in range(5):
        rows = ins[i].shape[0] // 2
        for h in range(2):
            some = pl.ds(h * rows, rows)
            out = outs[i].at[some] if i < 2 else outs[i].at[0, some]
            stores.append(pltpu.make_async_copy(ins[i].at[some], out, sem.at[2 * i + h]))
    for store in stores:
        store.start()
    for store in stores:
        store.wait()


def shards(activations, expert_ids, route_gates, gate_proj, up_proj, down_proj, cotangent):
    vmem = pl.BlockSpec(memory_space=pltpu.VMEM)
    anywhere = pl.BlockSpec(memory_space=pl.ANY)
    dma = pltpu.SemaphoreType.DMA
    tokens = jax.ShapeDtypeStruct((TOK, D), BF16)
    grads = jax.ShapeDtypeStruct((DC, FF), BF16)
    out = pl.pallas_call(
        kernel,
        out_shape=tuple(pltpu.VMEM(s.shape, BF16) for s in (tokens,) * 2 + (grads,) * 3),
        in_specs=[anywhere] * 9,
        out_specs=(vmem,) * 5,
        scratch_shapes=[
            pltpu.VMEM((TOP, TOK), jnp.int32),
            pltpu.VMEM((TOP, TOK), F32),
            pltpu.VMEM((TOK, D), BF16),
            pltpu.VMEM((TOK, D), BF16),
            pltpu.VMEM((D, FF), BF16),
            pltpu.VMEM((D, FF), BF16),
            pltpu.VMEM((D, FF), BF16),
            pltpu.VMEM((NP, GROUP * PIECE, 2 * GR), BF16),
            pltpu.VMEM((NP, 2 * GR, GROUP * PIECE), BF16),
            pltpu.VMEM((SLOTS, TOK), BF16),
            pltpu.VMEM((SLOTS, 1), F32),
            pltpu.VMEM((3, TOK, SLOTS), BF16),
            pltpu.VMEM((3, NE, NP, PIECE, QW), BF16),
            pltpu.VMEM((3, NE, NP, PIECE, QW), BF16),
            pltpu.VMEM((NE, 2 * NP, PIECE, DC), BF16),
            pltpu.VMEM((NE, 2 * NP, PIECE, DC), BF16),
            pltpu.VMEM((NG, NQ, GR, QW), BF16),
            pltpu.VMEM((SLOTS, D), BF16),
            pltpu.VMEM((SLOTS, D), BF16),
            pltpu.VMEM((2, ND, DC, SLOTS), BF16),
            pltpu.VMEM((2, SLOTS, FF), F32),
            pltpu.VMEM((3, 2, SLOTS, HALF), BF16),
            pltpu.VMEM((2, LINKS, 3, DC, HALF), BF16),
            pltpu.VMEM((2, LINKS, 3, DC, HALF), BF16),
            pltpu.VMEM((2, 2, DC, HALF), F32),
            dma((9,)),
            dma((4,)),
            dma((3,)),
            dma((NG + 2,)),
            dma((len(STAGES),)),
            dma((len(STAGES),)),
            dma,
            dma((2, 2, LINKS)),
        ],
        compiler_params=pltpu.CompilerParams(
            collective_id=0, has_side_effects=True, vmem_limit_bytes=57 * 2**20
        ),
        cost_estimate=pl.CostEstimate(flops=12 * 10**9, bytes_accessed=15 * 10**6, transcendentals=300000),
        name="expert_layer",
    )(expert_ids.T, route_gates.T, activations, cotangent, gate_proj, up_proj, down_proj, *constants())
    kept = jax.ShapeDtypeStruct((1, DC, FF), BF16)
    return pl.pallas_call(
        place,
        out_shape=(tokens,) * 2 + (kept,) * 3,
        in_specs=[vmem] * 5,
        out_specs=(anywhere,) * 5,
        scratch_shapes=[dma((10,))],
        compiler_params=pltpu.CompilerParams(vmem_limit_bytes=2**20),
        name="place",
    )(*out)


def solution(mesh):
    in_specs = (
        P(("dp", "expert"), None),
        P(("dp", "expert"), None),
        P(("dp", "expert"), None),
        P("expert", None, None),
        P("expert", None, None),
        P("expert", None, None),
        P(("dp", "expert"), None),
    )
    out_specs = (
        P(("dp", "expert"), None),
        P(("dp", "expert"), None),
        P("expert", "dp", None),
        P("expert", "dp", None),
        P("expert", "dp", None),
    )
    return jax.shard_map(shards, mesh=mesh, in_specs=in_specs, out_specs=out_specs, check_vma=False)
```
